128 devices in a mesh: ctx: 32 (over y, x, z_hi), tp: 4 (over z_lo, core).
Axes of the slice: x: 4, y: 4, z: 4 (z_hi: 2, z_lo: 2; z = z_hi * 2 + z_lo), core: 2. Of those that a mesh axis runs over, the one named last changes fastest.
Arguments:
- prompt_states: bfloat16 [16384, 1024], P('ctx', 'tp'), may hold values from -6 to 6
- scorer_gain: float32 [1024], replicated, may hold values from 0.1 to 1.9
- scorer_query: bfloat16 [1024, 2048], P(None, 'tp'), may hold values from -0.1875 to 0.1875
- scorer_key: bfloat16 [1024, 1024], P(None, 'tp'), may hold values from -0.1875 to 0.1875
- scorer_value: bfloat16 [1024, 1024], P(None, 'tp'), may hold values from -0.1875 to 0.1875
- scorer_querynorm: float32 [128], replicated, as said below
- scorer_keynorm: float32 [128], replicated, as said below
- scorer_project: bfloat16 [2048, 1024], P('tp'), may hold values from -0.125 to 0.125
- target_embeds: bfloat16 [16384, 5120], P('ctx', 'tp'), may hold values from -6 to 6
- target_gain: float32 [5120], replicated, may hold values from 0.1 to 1.9
- target_query: bfloat16 [5120, 4096], P(None, 'tp'), may hold values from -0.078125 to 0.078125
- target_key: bfloat16 [5120, 1024], P(None, 'tp'), may hold values from -0.078125 to 0.078125
- target_value: bfloat16 [5120, 1024], P(None, 'tp'), may hold values from -0.078125 to 0.078125
- target_querynorm: float32 [128], replicated, as said below
- target_keynorm: float32 [128], replicated, as said below
- kept_rows: int32 [32, 192], P('ctx'), may hold values from 0 to 511, as said below
- kept_counts: int32 [32], P('ctx'), may hold values from 1 to 192, 3072 in all
- shard_order: int32 [32], replicated, may hold values from 0 to 31, as said below
Outputs:
- scorer_states: bfloat16 [16384, 1024], P('ctx', 'tp')
- target_context: bfloat16 [3072, 4096], P('ctx', 'tp')
The draws below stay inside these ranges and needn't reach their ends.
Inputs may be any that keep to these rules, and one draw needn't show every extreme that they name: `kept_rows`: each row holds 192 distinct row numbers of its shard's 512 tokens in rising order; the first kept_counts of them are the kept tokens. `kept_counts`: they sum to 3072. `shard_order`: A permutation of the shard numbers. `scorer_querynorm`: gains of the query head norm. `scorer_keynorm`: gains of the key head norm. `target_querynorm`: gains of the query head norm. `target_keynorm`: gains of the key head norm.
All inputs are finite; a program needn't handle non-finite values. No bound on the sum of `kept_counts` on one device may be relied on, other than what follows from the above.
Results may differ from the reference program's by a relative error of at most 0.017.
The reference program's roundings to bfloat16 on the way count: a program that leaves them out, or rounds other values in their place, can miss the bound.
Values may be sent and summed in bfloat16 or wider, within the bound.
No kernel may reach another device: no remote copies, remote signals or barrier semaphores. Data moves between devices by JAX's collectives and lax.ppermute only.
A program may use at most 192 MiB of HBM per device.

```python
import math
import jax
import jax.numpy as jnp
import numpy as np
from jax import lax

DS = 1024
DT = 5120
HEAD = 128
QH_S = 16
KVH_S = 8
QH_T = 32
KVH_T = 8
TOK_DEV = 512
CAP = 192
TOKENS = 16384
KEPT = 3072
N_CTX = 32


def spread_gains(key, lower, upper):
    return jnp.exp(jax.random.uniform(key, (HEAD,), jnp.float32, math.log(lower), math.log(upper)))


def draw_scorer_querynorm(key, part):
    key = jax.random.fold_in(key, 11)
    return spread_gains(key, 0.5, 2.5)


def draw_scorer_keynorm(key, part):
    key = jax.random.fold_in(key, 12)
    return spread_gains(key, 0.5, 2.5)


def draw_target_querynorm(key, part):
    key = jax.random.fold_in(key, 13)
    return spread_gains(key, 0.5, 2.5)


def draw_target_keynorm(key, part):
    key = jax.random.fold_in(key, 14)
    return spread_gains(key, 0.5, 2.5)


def draw_kept_rows(key, part):
    key = jax.random.fold_in(key, 7)
    shard_keys = jax.random.split(key, N_CTX)

    def one(sub):
        order = jax.random.permutation(sub, TOK_DEV).astype(jnp.int32)
        ranked = order.at[0].set(TOK_DEV).at[TOK_DEV - 1].set(TOK_DEV + 1)
        chosen = lax.top_k(ranked, CAP)[1]
        return jnp.sort(chosen).astype(jnp.int32)
    return jax.vmap(one)(shard_keys)


def draw_shard_order(key, part):
    key = jax.random.fold_in(key, 21)
    mixed = jax.random.permutation(key, N_CTX).astype(jnp.int32)
    middle = N_CTX // 2
    where_middle = jnp.sum(jnp.where(mixed == middle, jnp.arange(N_CTX, dtype=jnp.int32), 0)).astype(jnp.int32)
    front = mixed[0]
    return mixed.at[where_middle].set(front).at[0].set(middle).astype(jnp.int32)


def shard_levels(stream_key, shape, cuts, low, high):
    def one(axis_at, parts):
        heights = jax.random.uniform(jax.random.fold_in(jax.random.fold_in(stream_key, 6), axis_at), (parts,), jnp.float32, low / len(cuts), high / len(cuts))
        return jnp.repeat(jnp.exp(heights), shape[axis_at] // parts).reshape((-1,) + (1,) * (len(shape) - axis_at - 1))

    loudness = one(*cuts[0])
    for cut in cuts[1:]:
        loudness = loudness * one(*cut)
    return loudness


def length_profile(number_of, total, limit, skew):
    weights = [(1 << 20) // math.isqrt(standing ** skew) + 1 for standing in range(2, number_of + 1)]
    surplus, holding = total - limit - (number_of - 1), [1] * (number_of - 1)
    while surplus > 0:
        free = [i for i in range(number_of - 1) if holding[i] < limit]
        mass, budget = sum([weights[i] for i in free]), surplus
        for i in free:
            extra = min(limit - holding[i], max(1, budget * weights[i] // mass), surplus)
            holding[i] = holding[i] + extra
            surplus = surplus - extra
    return np.array([limit] + holding)


def ragged(own_key, count, total, most, lean):
    if count == 2:
        one = jax.random.randint(own_key, (), max(1, total - most), min(most, total - 1) + 1)
        return jnp.stack([one, total - one])
    sizes = jnp.asarray(length_profile(count, total, most, lean), jnp.int32)
    pairs = (count - 1) // 2
    donor, receiver = sizes[1:1 + 2 * pairs:2], sizes[2:2 + 2 * pairs:2]
    margin = jnp.minimum(donor - 1, most - receiver)
    passed = jax.random.randint(jax.random.fold_in(own_key, 1), (pairs,), 0, 1 << 20) % (margin + 1)
    sizes = sizes.at[1:1 + 2 * pairs:2].set(donor - passed).at[2:2 + 2 * pairs:2].set(receiver + passed)
    return sizes[jax.random.permutation(jax.random.fold_in(own_key, 2), count)]


def normal_values(key, extent, spread, most, shards=(), held_as=jnp.bfloat16):
    values = spread * jax.random.normal(key, extent, jnp.float32)
    if shards:
        values = values * shard_levels(key, extent, shards, -0.22, 0.18)
    return jnp.clip(values, -most, most).astype(held_as)


def setup_inputs(seed: int = 0) -> dict:
    key_list = jax.random.split(jax.random.key(seed), 19)
    return {
        "prompt_states": normal_values(key_list[0], (TOKENS, DS), 1.0, 6.0, ((0, 32), (1, 4))),
        "scorer_gain": jnp.clip(1.0 + 0.18 * jax.random.normal(key_list[1], (DS,), jnp.float32), 0.1, 1.9),
        "scorer_query": normal_values(key_list[2], (DS, QH_S * HEAD), DS ** -0.5, 0.1875, ((1, 4),)),
        "scorer_key": normal_values(key_list[3], (DS, KVH_S * HEAD), DS ** -0.5, 0.1875, ((1, 4),)),
        "scorer_value": normal_values(key_list[4], (DS, KVH_S * HEAD), DS ** -0.5, 0.1875, ((1, 4),)),
        "scorer_querynorm": draw_scorer_querynorm(jax.random.fold_in(key_list[18], 71), 0),
        "scorer_keynorm": draw_scorer_keynorm(jax.random.fold_in(key_list[18], 71), 0),
        "scorer_project": normal_values(key_list[7], (QH_S * HEAD, DS), (QH_S * HEAD) ** -0.5, 0.125, ((0, 4),)),
        "target_embeds": normal_values(key_list[8], (TOKENS, DT), 1.0, 6.0, ((0, 32), (1, 4))),
        "target_gain": jnp.clip(1.0 + 0.18 * jax.random.normal(key_list[9], (DT,), jnp.float32), 0.1, 1.9),
        "target_query": normal_values(key_list[10], (DT, QH_T * HEAD), DT ** -0.5, 0.078125, ((1, 4),)),
        "target_key": normal_values(key_list[11], (DT, KVH_T * HEAD), DT ** -0.5, 0.078125, ((1, 4),)),
        "target_value": normal_values(key_list[12], (DT, KVH_T * HEAD), DT ** -0.5, 0.078125, ((1, 4),)),
        "target_querynorm": draw_target_querynorm(jax.random.fold_in(key_list[18], 71), 0),
        "target_keynorm": draw_target_keynorm(jax.random.fold_in(key_list[18], 71), 0),
        "kept_rows": draw_kept_rows(jax.random.fold_in(key_list[18], 71), 0),
        "kept_counts": ragged(key_list[16], N_CTX, KEPT, CAP, 2).astype(jnp.int32),
        "shard_order": draw_shard_order(jax.random.fold_in(key_list[18], 71), 0),
    }


EPS = 1e-06
ROPE_BASE = 1000000.0
NEG = -1e+30

def rms_scale(values, gain):
    mean_square = lax.optimization_barrier(jnp.mean(values * values, axis=-1, keepdims=True))
    return values * lax.rsqrt(mean_square + EPS) * gain

def rotate(values, positions):
    width = values.shape[-1]
    half = width // 2
    freqs = ROPE_BASE ** (jnp.arange(half, dtype=jnp.float32) * (-2.0 / width))
    angles = positions[:, None] * freqs[None, :]
    cosine = jnp.cos(angles)[:, None, :]
    sine = jnp.sin(angles)[:, None, :]
    first = values[..., :half]
    second = values[..., half:]
    return jnp.concatenate([first * cosine - second * sine, second * cosine + first * sine], axis=-1)

def heads_of(normed, weight, gain, positions):
    head = gain.shape[0]
    mixed = jnp.dot(normed, weight, preferred_element_type=jnp.float32)
    mixed = mixed.reshape(normed.shape[0], weight.shape[1] // head, head)
    return rotate(rms_scale(mixed, gain), positions).astype(jnp.bfloat16)

def causal_attention(queries, keys, values):
    count, heads, head = queries.shape
    groups = keys.shape[1]
    block = math.gcd(count, 256)
    grouped = queries.reshape(count, groups, heads // groups, head).astype(jnp.float32)
    keys_wide = keys.astype(jnp.float32)
    values_wide = values.astype(jnp.float32)
    key_pos = jnp.arange(count, dtype=jnp.int32)

    def one(start):
        rows = lax.dynamic_slice_in_dim(grouped, start, block, 0)
        query_pos = start + jnp.arange(block, dtype=jnp.int32)
        scores = jnp.einsum('rkgd,skd->kgrs', rows, keys_wide) * head ** (-0.5)
        allowed = key_pos[None, :] <= query_pos[:, None]
        masked = jnp.where(allowed, scores, NEG)
        top = lax.optimization_barrier(jnp.max(masked, axis=-1, keepdims=True))
        weights = jnp.where(allowed, jnp.exp(masked - top), 0.0)
        totals = lax.optimization_barrier(jnp.sum(weights, axis=-1))
        rounded = lax.optimization_barrier(weights.astype(jnp.bfloat16))
        mixed = jnp.einsum('kgrs,skd->kgrd', rounded.astype(jnp.float32), values_wide)
        out = mixed / totals[..., None]
        return jnp.transpose(out, (2, 0, 1, 3)).reshape(block, heads * head)
    starts = jnp.arange(count // block, dtype=jnp.int32) * block
    return lax.map(one, starts).reshape(count, heads * head).astype(jnp.bfloat16)

def layer_attention(states, gain, w_query, w_key, w_value, query_gain, key_gain):
    count = states.shape[0]
    head = query_gain.shape[0]
    positions = jnp.arange(count, dtype=jnp.int32).astype(jnp.float32)
    normed = rms_scale(states.astype(jnp.float32), gain).astype(jnp.bfloat16)
    queries = heads_of(normed, w_query, query_gain, positions)
    keys = heads_of(normed, w_key, key_gain, positions)
    values = jnp.dot(normed, w_value, preferred_element_type=jnp.float32).astype(jnp.bfloat16)
    values = values.reshape(count, w_value.shape[1] // head, head)
    return causal_attention(queries, keys, values)

def reference(prompt_states, scorer_gain, scorer_query, scorer_key, scorer_value, scorer_querynorm, scorer_keynorm, scorer_project, target_embeds, target_gain, target_query, target_key, target_value, target_querynorm, target_keynorm, kept_rows, kept_counts, shard_order):
    attended = layer_attention(prompt_states, scorer_gain, scorer_query, scorer_key, scorer_value, scorer_querynorm, scorer_keynorm)
    scorer_states = jnp.dot(attended, scorer_project, preferred_element_type=jnp.float32).astype(jnp.bfloat16)
    counts = kept_counts.astype(jnp.int32)
    shard_ids = jnp.arange(N_CTX, dtype=jnp.int32)
    ranks = lax.optimization_barrier(jnp.sum(jnp.where(shard_order.astype(jnp.int32)[:, None] == shard_ids[None, :], shard_ids[:, None], 0), axis=0)).astype(jnp.int32)
    earlier = ranks[None, :] < ranks[:, None]
    offsets = lax.optimization_barrier(jnp.sum(jnp.where(earlier, counts[None, :], 0), axis=1)).astype(jnp.int32)
    slots = jnp.arange(CAP, dtype=jnp.int32)
    dest = jnp.where(slots[None, :] < counts[:, None], offsets[:, None] + slots[None, :], KEPT).astype(jnp.int32)
    source = (shard_ids[:, None] * TOK_DEV + kept_rows.astype(jnp.int32)).reshape(-1)
    compressed = jnp.zeros((KEPT, DT), jnp.bfloat16).at[dest.reshape(-1)].set(target_embeds[source], mode='drop')
    target_context = layer_attention(compressed, target_gain, target_query, target_key, target_value, target_querynorm, target_keynorm)
    return (scorer_states, target_context)
```

```python
import jax
import jax.numpy as jnp
import numpy as np
from jax import lax
from jax.experimental import pallas as pl
from jax.experimental.pallas import tpu as pltpu
from jax.sharding import Mesh
from jax.sharding import PartitionSpec as P

F32 = jnp.float32
BF16 = jnp.bfloat16
EPS = 1e-06
ROPE_BASE = 1000000.0
NEG = -1e30
HEAD = 128
EXP_SCALE = float(HEAD**-0.5 * np.log2(np.e))
CTX = ("y", "x", "zh")
TP = ("zl", "c")
VMEM = pl.BlockSpec(memory_space=pltpu.VMEM)
SMEM = pl.BlockSpec(memory_space=pltpu.SMEM)
NN = (((1,), (0,)), ((), ()))
NT = (((1,), (1,)), ((), ()))


def shift(value, axis, size, by):
    return lax.ppermute(value, axis, [(i, (i + by) % size) for i in range(size)])


def rope_tables(positions):
    freqs = ROPE_BASE ** (jnp.arange(HEAD // 2, dtype=F32) * (-2.0 / HEAD))
    angles = positions.astype(F32)[:, None] * freqs[None, :]
    cosine, sine = jnp.cos(angles), jnp.sin(angles)
    return jnp.concatenate([cosine, cosine], axis=1), jnp.concatenate([-sine, sine], axis=1)


def head_rope(values, gain, cosine, sine):
    mean_square = jnp.mean(values * values, axis=-1, keepdims=True)
    normed = values * lax.rsqrt(mean_square + EPS) * gain
    return normed * cosine + pltpu.roll(normed, HEAD // 2, 1) * sine


def in_order(blocks, zl, c):
    b0, b1, b2, b3 = blocks
    first, second = jnp.where(c == 0, b0, b1), jnp.where(c == 0, b1, b0)
    third, fourth = jnp.where(c == 0, b2, b3), jnp.where(c == 0, b3, b2)
    low, high = zl == 0, zl != 0
    return (
        jnp.where(low, first, third),
        jnp.where(low, second, fourth),
        jnp.where(high, first, third),
        jnp.where(high, second, fourth),
    )


def scorer_qkv_kernel(
    place_ref, b0, b1, b2, b3, gain_ref, wq_ref, wg_ref, qg_ref, kg_ref, cos_ref, sin_ref, q_out, g_out
):
    zl, c = place_ref[0], place_ref[1]
    step = 128
    for part in range(b0.shape[0] // step):
        rows = slice(part * step, (part + 1) * step)
        blocks = in_order([b[rows, :].astype(F32) for b in (b0, b1, b2, b3)], zl, c)
        states = jnp.concatenate(blocks, axis=1)
        mean_square = jnp.mean(states * states, axis=-1, keepdims=True)
        normed = (states * lax.rsqrt(mean_square + EPS) * gain_ref[...]).astype(BF16)
        cosine, sine = cos_ref[rows, :], sin_ref[rows, :]
        queries = lax.dot_general(normed, wq_ref[...], NN, preferred_element_type=F32)
        other = lax.dot_general(normed, wg_ref[...], NN, preferred_element_type=F32)
        for h in range(4):
            lanes = slice(h * HEAD, (h + 1) * HEAD)
            turned = head_rope(queries[:, lanes], qg_ref[...], cosine, sine)
            q_out[h, rows, :] = turned.T.astype(BF16)
        for h in range(4):
            lanes = slice(h * HEAD, (h + 1) * HEAD)
            key = head_rope(other[:, lanes], kg_ref[...], cosine, sine)
            value = other[:, lanes].T
            g_out[h, rows, :] = jnp.where(c == 0, key, value).astype(BF16)


def scorer_qkv(place, blocks, gain, wq, wg, query_gain, key_gain, cosine, sine):
    rows = blocks[0].shape[0]
    shape = jax.ShapeDtypeStruct((4, rows, HEAD), BF16)
    return pl.pallas_call(
        scorer_qkv_kernel,
        out_shape=[shape, shape],
        in_specs=[SMEM] + [VMEM] * 11,
        out_specs=[VMEM] * 2,
        compiler_params=pltpu.CompilerParams(vmem_limit_bytes=32 << 20),
        cost_estimate=pl.CostEstimate(
            flops=2 * rows * 1024 * 1024, bytes_accessed=4 << 20, transcendentals=0
        ),
        name="scorer_qkv",
    )(place, *blocks, gain, wq, wg, query_gain, key_gain, cosine, sine)


def attend_kernel(first, last, *refs):
    place_ref, q_ref, own_ref, other_ref = refs[:4]
    refs = refs[4:]
    if first:
        carried = None
    else:
        carried, refs = refs[:3], refs[3:]
    if last:
        out_ref, refs = refs[0], refs[1:]
    m_ref, l_ref, a_ref = refs[:3]
    k_ref, vt_ref = refs[3:]
    relation, y, c = place_ref[0], place_ref[1], place_ref[2]
    size = q_ref.shape[1]
    pieces = size // HEAD
    for block in range(4):
        slot = lax.rem(y - block + 4, 4)
        own, other = own_ref[slot], other_ref[slot]
        k_ref[block] = jnp.where(c == 0, own, other)
        value = jnp.where(c == 0, other, own)
        vt_ref[block] = jnp.concatenate(
            [value[i * HEAD : (i + 1) * HEAD] for i in range(pieces)], axis=1
        )

    def query(block):
        tiles = q_ref[lax.rem(y - block + 4, 4)]
        return jnp.concatenate([tiles[i * HEAD : (i + 1) * HEAD] for i in range(pieces)], axis=1)

    queries = [query(block) for block in range(4)]

    def scores(pair):
        return lax.dot_general(k_ref[pair[1]], queries[pair[0]], NN, preferred_element_type=F32)

    def run(pairs, source, masked):
        state = {}
        ahead = scores(pairs[0])
        for at, (block, keys) in enumerate(pairs):
            s = ahead
            if at + 1 < len(pairs):
                ahead = scores(pairs[at + 1])
            if masked and block == keys:
                key_at = lax.broadcasted_iota(jnp.int32, s.shape, 0)
                query_at = lax.broadcasted_iota(jnp.int32, s.shape, 1)
                s = jnp.where(key_at <= query_at, s, NEG)
            if block not in state and source is not None:
                state[block] = tuple(ref[block] for ref in source)
            top = jnp.max(s, axis=0, keepdims=True)
            if block in state:
                m, l, a = state[block]
                fresh = jnp.maximum(m, top)
                shrink = jnp.exp2((m - fresh) * EXP_SCALE)
            else:
                fresh = top
            weights = jnp.exp2(s * EXP_SCALE - fresh * EXP_SCALE)
            total = jnp.sum(weights, axis=0, keepdims=True)
            added = lax.dot_general(
                vt_ref[keys], weights.astype(BF16), NN, preferred_element_type=F32
            )
            if block in state:
                total, added = l * shrink + total, a * shrink + added
            state[block] = (fresh, total, added)
        for block, values in state.items():
            m_ref[block], l_ref[block], a_ref[block] = values

    earlier = [(block, keys) for block in range(4) for keys in range(block)]
    same = [(block, block) for block in range(4)]
    if first:
        run(sorted(earlier + same), None, True)
    else:
        for ref, out in zip(carried, (m_ref, l_ref, a_ref)):
            out[0] = ref[0]
        run(earlier, carried, False)

        @pl.when(relation > 0)
        def _():
            run(same, (m_ref, l_ref, a_ref), False)

    if last:
        for block in range(4):
            out_ref[block] = (a_ref[block] / l_ref[block]).T.astype(BF16)


def attend(first, last, place, queries, own, other, carry):
    size = queries.shape[1]
    state = [(4, 1, size), (4, 1, size), (4, HEAD, size)]
    shapes = [jax.ShapeDtypeStruct(s, F32) for s in state]
    scratch = [pltpu.VMEM((4, size, HEAD), BF16), pltpu.VMEM((4, HEAD, size), BF16)]
    if last:
        out_shape = jax.ShapeDtypeStruct((4, size, HEAD), BF16)
        scratch = [pltpu.VMEM(s, F32) for s in state] + scratch
        aliases = {}
    else:
        out_shape = shapes
        aliases = {} if first else {4: 0, 5: 1, 6: 2}
    carry = () if first else carry

    def kernel(*refs):
        attend_kernel(first, last, *refs)

    return pl.pallas_call(
        kernel,
        out_shape=out_shape,
        in_specs=[SMEM] + [VMEM] * (3 + len(carry)),
        out_specs=VMEM if last else [VMEM] * 3,
        scratch_shapes=scratch,
        input_output_aliases=aliases,
        compiler_params=pltpu.CompilerParams(vmem_limit_bytes=48 << 20),
        cost_estimate=pl.CostEstimate(
            flops=8 * 4 * size * size * HEAD * 2, bytes_accessed=4 << 20, transcendentals=8 * size * size
        ),
        name="scorer_attend",
    )(place, queries, own, other, *carry)


def target_qkv_kernel(
    place_ref, b0, b1, b2, b3, gain_ref, qg_ref, kg_ref, cos_ref, sin_ref, wq_ref, wk_ref, wv_ref,
    q_out, kv_out, normed_ref, q_acc, k_acc, v_acc,
):
    at = pl.program_id(0)
    steps = pl.num_programs(0)
    rows, part = b0.shape
    block = wq_ref.shape[0]

    @pl.when(at == 0)
    def _():
        blocks = in_order([b[...].astype(F32) for b in (b0, b1, b2, b3)], place_ref[0], place_ref[1])
        total = sum(jnp.sum(b * b, axis=-1, keepdims=True) for b in blocks)
        factor = lax.rsqrt(total / (4 * part) + EPS)
        for index in range(4):
            normed = blocks[index] * factor * gain_ref[:, index * part : (index + 1) * part]
            normed = normed.astype(BF16)
            for piece in range(part // block):
                normed_ref[index * (part // block) + piece] = normed[
                    :, piece * block : (piece + 1) * block
                ]
        q_acc[...] = jnp.zeros_like(q_acc)
        k_acc[...] = jnp.zeros_like(k_acc)
        v_acc[...] = jnp.zeros_like(v_acc)

    normed = normed_ref[at]
    q_acc[...] += lax.dot_general(normed, wq_ref[...], NN, preferred_element_type=F32)
    k_acc[...] += lax.dot_general(normed, wk_ref[...], NN, preferred_element_type=F32)
    v_acc[...] += lax.dot_general(normed, wv_ref[...], NN, preferred_element_type=F32)

    @pl.when(at == steps - 1)
    def _():
        cosine, sine = cos_ref[...], sin_ref[...]
        for h in range(8):
            turned = head_rope(q_acc[:, h * HEAD : (h + 1) * HEAD], qg_ref[...], cosine, sine)
            q_out[h // 4, (h % 4) * rows : (h % 4 + 1) * rows, :] = turned.astype(BF16)
        for h in range(2):
            lanes = slice(h * HEAD, (h + 1) * HEAD)
            turned = head_rope(k_acc[:, lanes], kg_ref[...], cosine, sine)
            kv_out[:, lanes] = turned.astype(BF16)
        kv_out[:, 2 * HEAD :] = v_acc[...].astype(BF16)


def target_qkv(place, blocks, gain, query_gain, key_gain, cosine, sine, wq, wk, wv):
    rows, part = blocks[0].shape
    block = 640
    steps = 4 * part // block
    whole = lambda shape: pl.BlockSpec(shape, lambda i: (0,) * len(shape))
    return pl.pallas_call(
        target_qkv_kernel,
        grid=(steps,),
        out_shape=[
            jax.ShapeDtypeStruct((2, 4 * rows, HEAD), BF16),
            jax.ShapeDtypeStruct((rows, 4 * HEAD), BF16),
        ],
        in_specs=[SMEM]
        + [whole((rows, part))] * 4
        + [whole(gain.shape), whole((1, HEAD)), whole((1, HEAD)), whole((rows, HEAD)), whole((rows, HEAD))]
        + [
            pl.BlockSpec((block, wq.shape[1]), lambda i: (i, 0)),
            pl.BlockSpec((block, wk.shape[1]), lambda i: (i, 0)),
            pl.BlockSpec((block, wv.shape[1]), lambda i: (i, 0)),
        ],
        out_specs=[whole((2, 4 * rows, HEAD)), whole((rows, 4 * HEAD))],
        scratch_shapes=[
            pltpu.VMEM((steps, rows, block), BF16),
            pltpu.VMEM((rows, wq.shape[1]), F32),
            pltpu.VMEM((rows, wk.shape[1]), F32),
            pltpu.VMEM((rows, wv.shape[1]), F32),
        ],
        compiler_params=pltpu.CompilerParams(vmem_limit_bytes=32 << 20),
        cost_estimate=pl.CostEstimate(
            flops=2 * rows * 4 * part * 1536, bytes_accessed=16 << 20, transcendentals=0
        ),
        name="target_qkv",
    )(place, *blocks, gain, query_gain, key_gain, cosine, sine, wq, wk, wv)


def target_attend_kernel(place_ref, q_ref, c0, c1, c2, c3, out_ref, m_ref, l_ref, a_ref):
    y, first = place_ref[0], place_ref[1]
    members = 4
    rows = q_ref.shape[1] // members

    def chunk(keys_ref, own):
        for g in range(2):
            keys = keys_ref[:, g * HEAD : (g + 1) * HEAD]
            values = keys_ref[:, (2 + g) * HEAD : (3 + g) * HEAD]
            s = lax.dot_general(q_ref[g], keys, NT, preferred_element_type=F32)
            if own:
                row = lax.broadcasted_iota(jnp.int32, (rows, s.shape[1]), 0) + first
                key_at = lax.broadcasted_iota(jnp.int32, (rows, s.shape[1]), 1)
                allowed = jnp.concatenate([key_at <= row] * members, axis=0)
                s = jnp.where(allowed, s, NEG)
            fresh = jnp.max(s, axis=1, keepdims=True)
            if not own:
                m = m_ref[g]
                fresh = jnp.maximum(m, fresh)
                shrink = jnp.exp2((m - fresh) * EXP_SCALE)
            weights = jnp.exp2(s * EXP_SCALE - fresh * EXP_SCALE)
            total = jnp.sum(weights, axis=1, keepdims=True)
            added = lax.dot_general(weights.astype(BF16), values, NN, preferred_element_type=F32)
            if not own:
                total, added = l_ref[g] * shrink + total, a_ref[g] * shrink + added
            m_ref[g], l_ref[g], a_ref[g] = fresh, total, added

    chunk(c0, True)
    for by, ref in ((1, c1), (2, c2), (3, c3)):

        @pl.when(y >= by)
        def _():
            chunk(ref, False)

    for g in range(2):
        context = (a_ref[g] / l_ref[g]).astype(BF16)
        for member in range(members):
            lanes = slice((g * members + member) * HEAD, (g * members + member + 1) * HEAD)
            out_ref[:, lanes] = context[member * rows : (member + 1) * rows]


def target_attend(place, queries, chunks):
    groups, many, _ = queries.shape
    rows = many // 4
    return pl.pallas_call(
        target_attend_kernel,
        out_shape=jax.ShapeDtypeStruct((rows, 8 * HEAD), BF16),
        in_specs=[SMEM] + [VMEM] * 5,
        out_specs=VMEM,
        scratch_shapes=[
            pltpu.VMEM((groups, many, 1), F32),
            pltpu.VMEM((groups, many, 1), F32),
            pltpu.VMEM((groups, many, HEAD), F32),
        ],
        compiler_params=pltpu.CompilerParams(vmem_limit_bytes=32 << 20),
        cost_estimate=pl.CostEstimate(
            flops=4 * many * 2 * 3072 * HEAD, bytes_accessed=4 << 20, transcendentals=many * 6144
        ),
        name="target_attend",
    )(place, queries, *chunks)


def gather_tp(value):
    chip = shift(value, "zl", 2, 1)
    return [value, shift(value, "c", 2, 1), chip, shift(chip, "c", 2, 1)]


def swap_heads(weight, c):
    even, odd = weight[0::2], weight[1::2]
    keep = jnp.where(c == 0, even, odd)
    got = shift(jnp.where(c == 0, odd, even), "c", 2, 1)
    return jnp.where(c == 0, jnp.concatenate([keep, got]), jnp.concatenate([got, keep]))


def exchange_y(blocks, y):
    got = [lax.dynamic_index_in_dim(blocks, y, 0, keepdims=False)]
    for by in (1, 3, 2):
        got.append(
            shift(lax.dynamic_index_in_dim(blocks, lax.rem(y + by, 4), 0, keepdims=False), "y", 4, by)
        )
    return [got[0], got[1], got[3], got[2]]


def on_device(
    prompt_states,
    scorer_gain,
    scorer_query,
    scorer_key,
    scorer_value,
    scorer_querynorm,
    scorer_keynorm,
    scorer_project,
    target_embeds,
    target_gain,
    target_query,
    target_key,
    target_value,
    target_querynorm,
    target_keynorm,
    kept_rows,
    kept_counts,
    shard_order,
):
    y, x, zh, zl, c = (lax.axis_index(name) for name in ("y", "x", "zh", "zl", "c"))
    place = (y * 4 + x) * 2 + zh
    tp_place = jnp.stack([zl, c]).astype(jnp.int32)
    rows = prompt_states.shape[0]

    state_blocks = gather_tp(prompt_states)
    width = prompt_states.shape[1] * 4
    wq = swap_heads(scorer_query.reshape(width, 4, HEAD).transpose(1, 0, 2), c)
    wq = wq.transpose(1, 0, 2).reshape(width, 4 * HEAD)
    keep = jnp.where(c == 0, scorer_key, scorer_value)
    got = shift(jnp.where(c == 0, scorer_value, scorer_key), "c", 2, 1)
    wg = jnp.where(c == 0, jnp.concatenate([keep, got], 1), jnp.concatenate([got, keep], 1))
    wp = swap_heads(scorer_project.reshape(4, HEAD, width), c)
    wp = jnp.take(wp, lax.rem(y - jnp.arange(4) + 4, 4), axis=0).reshape(4 * HEAD, width)
    cosine, sine = rope_tables(place * rows + jnp.arange(rows, dtype=jnp.int32))
    queries, shared = scorer_qkv(
        tp_place, state_blocks, scorer_gain[None], wq, wg,
        scorer_querynorm[None], scorer_keynorm[None], cosine, sine,
    )
    own = jnp.stack(exchange_y(shared, y))
    queries = jnp.stack(exchange_y(queries, y))

    shards = shard_order.shape[0]
    capacity = kept_rows.shape[1]
    target_rows = capacity // 2
    counts = lax.all_to_all(jnp.broadcast_to(kept_counts[:, None], (shards, 1)), CTX, 0, 0, tiled=True)[:, 0]
    shard_ids = jnp.arange(shards, dtype=jnp.int32)
    ranks = jnp.sum(jnp.where(shard_order[:, None] == shard_ids[None, :], shard_ids[:, None], 0), axis=0)
    starts = jnp.sum(jnp.where(ranks[None, :] < ranks[:, None], counts[None, :], 0), axis=1)
    turns = capacity // shards
    my_start = jnp.sum(jnp.where(shard_ids == place, starts, 0))
    slot = (shard_ids[:, None] - my_start) % shards + shards * jnp.arange(turns, dtype=jnp.int32)[None, :]
    picked = jnp.take(kept_rows[0], slot.reshape(-1), axis=0)
    sent = jnp.take(target_embeds, picked, axis=0)
    features = target_embeds.shape[1]
    passed = lax.all_to_all(sent.reshape(shards, -1, 128), CTX, 0, 0, tiled=True)
    passed = passed.reshape(capacity, features)
    within = (place - starts[:, None]) % shards + shards * jnp.arange(turns, dtype=jnp.int32)[None, :]
    dest = jnp.where(within < counts[:, None], (starts[:, None] + within) // shards, -1).reshape(-1)
    select = (jnp.arange(target_rows, dtype=jnp.int32)[:, None] == dest[None, :]).astype(BF16)
    placed = jnp.dot(select, passed, preferred_element_type=F32).astype(BF16)
    landed = lax.all_to_all(placed.reshape(shards, -1, 128), CTX, 0, 0, tiled=True)
    compressed = landed.reshape(shards, target_rows // shards, features).transpose(1, 0, 2)
    compressed = compressed.reshape(target_rows, features)

    target_cos, target_sin = rope_tables(place * target_rows + jnp.arange(target_rows, dtype=jnp.int32))
    target_queries, target_kv = target_qkv(
        tp_place, gather_tp(compressed), target_gain[None], target_querynorm[None], target_keynorm[None],
        target_cos, target_sin, target_query, target_key, target_value,
    )
    other_kv = shift(target_kv, "zh", 2, 1)
    pair = jnp.where(
        zh == 0, jnp.concatenate([target_kv, other_kv]), jnp.concatenate([other_kv, target_kv])
    )
    line = jnp.stack([pair, shift(pair, "x", 4, 1), shift(pair, "x", 4, 2), shift(pair, "x", 4, 3)])
    line = jnp.take(line, lax.rem(x - jnp.arange(4) + 4, 4), axis=0).reshape(8 * target_rows, -1)
    chunks = [line] + [
        lax.ppermute(line, "y", [(i, i + by) for i in range(4 - by)]) for by in (1, 2, 3)
    ]

    me = 2 * x + zh
    zero = jnp.int32(0)

    def scalars(from_x, from_zh):
        return jnp.stack([me - (2 * from_x + from_zh), y, c]).astype(jnp.int32)

    across = shift(own, "zh", 2, 1)
    arrivals = [(own, x, zh)]
    arrivals.append((across, x, 1 - zh))
    for by in (1, 3, 2):
        arrivals.append((shift(own, "x", 4, by), lax.rem(x - by + 4, 4), zh))
    for by in (1, 3, 2):
        arrivals.append((shift(across, "x", 4, by), lax.rem(x - by + 4, 4), 1 - zh))
    carry = None
    for index, (chunk, from_x, from_zh) in enumerate(arrivals):
        swapped = shift(chunk, "c", 2, 1)
        carry = attend(
            index == 0, index == len(arrivals) - 1, scalars(from_x, from_zh), queries, chunk, swapped, carry
        )

    attended = jnp.concatenate(exchange_y(carry, y), axis=1)
    half, quarter = width // 2, width // 4
    away = lax.dynamic_slice_in_dim(wp, (1 - zl) * half, half, 1)
    home = lax.dynamic_slice_in_dim(wp, zl * half, half, 1)
    from_chip = shift(
        jnp.dot(attended, away, preferred_element_type=F32).astype(BF16), "zl", 2, 1
    ).astype(F32)
    mine = jnp.dot(attended, home, preferred_element_type=F32) + from_chip
    send = lax.dynamic_slice_in_dim(mine, (1 - c) * quarter, quarter, 1)
    stay = lax.dynamic_slice_in_dim(mine, c * quarter, quarter, 1)
    scorer_states = (stay + shift(send.astype(BF16), "c", 2, 1).astype(F32)).astype(BF16)

    target_place = jnp.stack([y, me * target_rows]).astype(jnp.int32)
    target_context = target_attend(target_place, target_queries, chunks)
    return (scorer_states, target_context)


def solution(mesh):
    fine = Mesh(mesh.devices.reshape(4, 4, 2, 2, 2), CTX + TP)
    return jax.shard_map(
        on_device,
        mesh=fine,
        in_specs=(
            P(CTX, TP),
            P(),
            P(None, TP),
            P(None, TP),
            P(None, TP),
            P(),
            P(),
            P(TP, None),
            P(CTX, TP),
            P(),
            P(None, TP),
            P(None, TP),
            P(None, TP),
            P(),
            P(),
            P(CTX, None),
            P(CTX),
            P(),
        ),
        out_specs=(P(CTX, TP), P(CTX, TP)),
        check_vma=False,
    )
```

```python
import jax
import jax.numpy as jnp
import numpy as np
from jax import lax
from jax.experimental import pallas as pl
from jax.experimental.pallas import tpu as pltpu
from jax.sharding import Mesh
from jax.sharding import PartitionSpec as P

F32 = jnp.float32
BF16 = jnp.bfloat16
EPS = 1e-06
ROPE_BASE = 1000000.0
NEG = -1e30
HEAD = 128
EXP_SCALE = float(HEAD**-0.5 * np.log2(np.e))
CTX = ("y", "x", "zh")
TP = ("zl", "c")
VMEM = pl.BlockSpec(memory_space=pltpu.VMEM)
SMEM = pl.BlockSpec(memory_space=pltpu.SMEM)
ANY = pl.BlockSpec(memory_space=pl.ANY)
LIMIT = 24 << 20
SCALE = 0.25


def cost(microseconds):
    return pl.CostEstimate(
        flops=int(microseconds * SCALE * 1.1e9), bytes_accessed=1024, transcendentals=0
    )
NN = (((1,), (0,)), ((), ()))
NT = (((1,), (1,)), ((), ()))


def shift(value, axis, size, by):
    return lax.ppermute(value, axis, [(i, (i + by) % size) for i in range(size)])


def rope_tables(positions):
    lane = jnp.arange(HEAD)
    freqs = ROPE_BASE ** ((lane % (HEAD // 2)).astype(F32) * (-2.0 / HEAD))
    angles = positions.astype(F32)[:, None] * freqs[None, :]
    return jnp.cos(angles), jnp.where(lane < HEAD // 2, -1.0, 1.0)[None, :] * jnp.sin(angles)


def head_rope(values, gain, cosine, sine):
    mean_square = jnp.mean(values * values, axis=-1, keepdims=True)
    normed = values * lax.rsqrt(mean_square + EPS) * gain
    return normed * cosine + pltpu.roll(normed, HEAD // 2, 1) * sine


def in_order(blocks, zl, c):
    b0, b1, b2, b3 = blocks
    first, second = jnp.where(c == 0, b0, b1), jnp.where(c == 0, b1, b0)
    third, fourth = jnp.where(c == 0, b2, b3), jnp.where(c == 0, b3, b2)
    low, high = zl == 0, zl != 0
    return (
        jnp.where(low, first, third),
        jnp.where(low, second, fourth),
        jnp.where(high, first, third),
        jnp.where(high, second, fourth),
    )


def scorer_qkv_kernel(
    place_ref, b0, b1, b2, b3, gain_ref, wq_ref, wk_ref, wv_ref, gq_ref, gkv_ref,
    qg_ref, kg_ref, cos_ref, sin_ref, after_ref, out_ref, w_ref, normed_ref,
):
    zl, c = place_ref[0], place_ref[1]
    pair = 2 * HEAD
    for i in range(2):
        mine, got = (
            jnp.where(
                c == 0,
                ref[:, 2 * i * HEAD : (2 * i + 1) * HEAD],
                ref[:, (2 * i + 1) * HEAD : (2 * i + 2) * HEAD],
            )
            for ref in (wq_ref, gq_ref)
        )
        w_ref[:, i * HEAD : (i + 1) * HEAD] = jnp.where(c == 0, mine, got)
        w_ref[:, pair + i * HEAD : pair + (i + 1) * HEAD] = jnp.where(c == 0, got, mine)
    for i, own_ref in ((1, wk_ref), (2, wv_ref)):
        own, got = own_ref[...], gkv_ref[:, (i - 1) * pair : i * pair]
        w_ref[:, 2 * i * pair : (2 * i + 1) * pair] = jnp.where(c == 0, own, got)
        w_ref[:, (2 * i + 1) * pair : (2 * i + 2) * pair] = jnp.where(c == 0, got, own)
    step, many = 128, b0.shape[0]
    half = many // 2
    for part in range(many // step):
        rows = slice(part * step, (part + 1) * step)
        blocks = in_order([b[rows, :].astype(F32) for b in (b0, b1, b2, b3)], zl, c)
        states = jnp.concatenate(blocks, axis=1)
        mean_square = jnp.mean(states * states, axis=-1, keepdims=True)
        normed = (states * lax.rsqrt(mean_square + EPS) * gain_ref[...]).astype(BF16)
        normed_ref[rows, :] = normed
        mixed = lax.dot_general(normed, w_ref[:, : 2 * pair], NN, preferred_element_type=F32)
        for h in range(4):
            turned = head_rope(
                mixed[:, h * HEAD : (h + 1) * HEAD], qg_ref[...], cos_ref[rows, :], sin_ref[rows, :]
            )
            out_ref[h, many + part * step : many + (part + 1) * step, :] = turned.T.astype(BF16)
    for part in range(half // step):
        rows = pl.ds(pl.multiple_of(c * half + part * step, step), step)
        mixed = lax.dot_general(
            normed_ref[rows, :], w_ref[:, 2 * pair :], NN, preferred_element_type=F32
        )
        for h in range(4):
            key = head_rope(
                mixed[:, h * HEAD : (h + 1) * HEAD], kg_ref[...], cos_ref[rows, :], sin_ref[rows, :]
            )
            out_ref[h, part * step : (part + 1) * step, :] = key.astype(BF16)
            value = mixed[:, (4 + h) * HEAD : (5 + h) * HEAD].T
            out_ref[h, half + part * step : half + (part + 1) * step, :] = value.astype(BF16)


def scorer_qkv(place, blocks, *rest):
    rows = blocks[0].shape[0]
    return pl.pallas_call(
        scorer_qkv_kernel,
        out_shape=jax.ShapeDtypeStruct((4, 2 * rows, HEAD), BF16),
        in_specs=[SMEM] + [VMEM] * (3 + len(rest)) + [ANY],
        out_specs=VMEM,
        scratch_shapes=[
            pltpu.VMEM((4 * blocks[0].shape[1], 12 * HEAD), BF16),
            pltpu.VMEM((rows, 4 * blocks[0].shape[1]), BF16),
        ],
        compiler_params=pltpu.CompilerParams(vmem_limit_bytes=LIMIT),
        cost_estimate=cost(7),
        name="scorer_qkv",
    )(place, *blocks, *rest)


def project_kernel(place_ref, a0, a1, a2, a3, w_ref, got_ref, *refs):
    away_out, home_out, pick_ref = refs[-3:]
    y, c = place_ref[0], place_ref[1]
    heads = [None] * 4
    for i in range(2):
        mine, got = (
            jnp.where(
                c == 0,
                ref[2 * i * HEAD : (2 * i + 1) * HEAD, :],
                ref[(2 * i + 1) * HEAD : (2 * i + 2) * HEAD, :],
            )
            for ref in (w_ref, got_ref)
        )
        heads[i] = jnp.where(c == 0, mine, got)
        heads[2 + i] = jnp.where(c == 0, got, mine)
    width = w_ref.shape[1] // 4
    for at in range(4):
        slot = lax.rem(y - at + 4, 4)
        for block in range(4):
            pick_ref[block, pl.ds(pl.multiple_of(slot * HEAD, HEAD), HEAD), :] = heads[at][
                :, block * width : (block + 1) * width
            ]
    attended = jnp.concatenate([a[...] for a in (a0, a1, a2, a3)], axis=1)
    for zl in range(2):
        away_out[zl] = lax.dot_general(
            attended, pick_ref[zl * 2 + 1 - c], NN, preferred_element_type=F32
        ).astype(BF16)
        home_out[zl] = lax.dot_general(attended, pick_ref[zl * 2 + c], NN, preferred_element_type=F32)


def project(place, attended, weight, got, after):
    rows, width = attended[0].shape[0], weight.shape[1] // 4
    return pl.pallas_call(
        project_kernel,
        out_shape=[
            jax.ShapeDtypeStruct((2, rows, width), BF16),
            jax.ShapeDtypeStruct((2, rows, width), F32),
        ],
        in_specs=[SMEM] + [VMEM] * 6 + [ANY] * len(after),
        out_specs=[VMEM] * 2,
        scratch_shapes=[pltpu.VMEM((4, 4 * HEAD, width), BF16)],
        compiler_params=pltpu.CompilerParams(vmem_limit_bytes=LIMIT),
        cost_estimate=cost(2.5),
        name="scorer_project",
    )(place, *attended, weight, got, *after)


SLOTS = 8


def route_kernel(place_ref, counts_ref, order_ref, rows_ref, embeds_ref, sent_out, select_out):
    place = place_ref[0]
    shards, capacity = counts_ref.shape[0], rows_ref.shape[1]
    turns, entries = capacity // shards, sent_out.shape[0]
    iota = lambda shape, axis: lax.broadcasted_iota(jnp.int32, shape, axis)
    square = (shards, shards)
    counts = counts_ref[...]
    eye = iota(square, 0) == iota(square, 1)
    rank_row = jnp.sum(
        jnp.where(order_ref[...] == iota(square, 1), iota(square, 0), 0), axis=0, keepdims=True
    )
    rank = jnp.sum(jnp.where(eye, rank_row, 0), axis=1, keepdims=True)
    count_row = jnp.sum(jnp.where(eye, counts, 0), axis=0, keepdims=True)
    starts = jnp.sum(jnp.where(rank_row < rank, count_row, 0), axis=1, keepdims=True)
    my_start = jnp.sum(jnp.where(iota((shards, 1), 0) == place, starts, 0))
    entry = iota((entries, 1), 0)
    slot = ((entry // SLOTS - my_start) & (shards - 1)) + shards * (entry % SLOTS)
    picked = jnp.sum(
        jnp.where(iota((entries, capacity), 1) == slot, rows_ref[...], 0), axis=1, keepdims=True
    )
    pick = jnp.where(iota((entries, embeds_ref.shape[0]), 1) == picked, 1.0, 0.0).astype(BF16)
    sent_out[...] = lax.dot_general(
        pick, embeds_ref[...], NN, preferred_element_type=F32
    ).astype(BF16)
    wide = (shards, entries)
    source = iota(wide, 0) == iota(wide, 1) // SLOTS
    start = jnp.sum(jnp.where(source, starts, 0), axis=0, keepdims=True)
    count = jnp.sum(jnp.where(source, counts, 0), axis=0, keepdims=True)
    turn = iota((1, entries), 1) % SLOTS
    within = ((place - start) & (shards - 1)) + shards * turn
    good = (within < count) & (turn < turns)
    turn_at = (start + within) // shards
    dest = jnp.where(good, turn_at // 3 * SLOTS + turn_at % 3, -1)
    select_out[...] = jnp.where(iota(select_out.shape, 0) == dest, 1.0, 0.0).astype(BF16)


def route(place, counts, order, rows, embeds):
    entries = rows.shape[0] * counts.shape[0] * SLOTS
    return pl.pallas_call(
        route_kernel,
        out_shape=[
            jax.ShapeDtypeStruct((entries, embeds.shape[1]), BF16),
            jax.ShapeDtypeStruct((entries, entries), BF16),
        ],
        in_specs=[SMEM] + [VMEM] * 4,
        out_specs=[VMEM] * 2,
        compiler_params=pltpu.CompilerParams(vmem_limit_bytes=LIMIT),
        cost_estimate=cost(1),
        name="route",
    )(place, counts, order, rows, embeds)


def place_kernel(select_ref, rows_ref, after_ref, out_ref):
    out_ref[...] = lax.dot_general(
        select_ref[...], rows_ref[...], NN, preferred_element_type=F32
    ).astype(BF16)


def land_kernel(rows_ref, after_ref, out_ref):
    shape = (out_ref.shape[0], rows_ref.shape[0])
    shards = shape[1] // SLOTS
    row, entry = lax.broadcasted_iota(jnp.int32, shape, 0), lax.broadcasted_iota(jnp.int32, shape, 1)
    wanted = (row % shards) * SLOTS + row // shards
    select = jnp.where(entry == wanted, 1.0, 0.0).astype(BF16)
    out_ref[...] = lax.dot_general(
        select, rows_ref[...], NN, preferred_element_type=F32
    ).astype(BF16)


def move(kernel, name, rows, *operands):
    return pl.pallas_call(
        kernel,
        out_shape=jax.ShapeDtypeStruct((rows, operands[-2].shape[1]), BF16),
        in_specs=[VMEM] * (len(operands) - 1) + [ANY],
        out_specs=VMEM,
        compiler_params=pltpu.CompilerParams(vmem_limit_bytes=LIMIT),
        cost_estimate=cost(0.5),
        name=name,
    )(*operands)


def split_kernel(b0, b1, b2, b3, after_ref, own_out, query_out):
    size = own_out.shape[1]
    for at, ref in enumerate((b0, b1, b2, b3)):
        own_out[at] = ref[:size, :]
        query_out[at] = ref[size:, :]


def split(blocks, after):
    size = blocks[0].shape[0] // 2
    return pl.pallas_call(
        split_kernel,
        out_shape=[jax.ShapeDtypeStruct((4, size, HEAD), BF16)] * 2,
        in_specs=[VMEM] * 4 + [ANY],
        out_specs=[VMEM] * 2,
        cost_estimate=cost(0.5),
        name="split",
    )(*blocks, after)


def attend_kernel(first, last, many, waits, *refs):
    place_ref, qa_ref, qb_ref = refs[:3]
    chunk_refs, refs = refs[3 : 3 + many], refs[3 + many :]
    carried = None
    if not first:
        carried, refs = refs[:3], refs[3:]
    refs = refs[waits:]
    if last:
        mine_out, *theirs_out = refs[:3]
        refs = refs[3:]
    m_ref, l_ref, a_ref, k_ref, vt_ref, q_ref = refs
    y, c = place_ref[0], place_ref[1]
    size = qa_ref.shape[1]
    half = size // 2
    wide = half * many
    for block in range(4):
        slot = lax.rem(y - block + 4, 4)
        for at, ref in enumerate(chunk_refs):
            chunk = ref[slot]
            k_ref[(block * many + at) * half : (block * many + at + 1) * half, :] = chunk[:half]
            for i in range(half // HEAD):
                lanes = (block * many + at) * half + i * HEAD
                vt_ref[:, lanes : lanes + HEAD] = chunk[half + i * HEAD : half + (i + 1) * HEAD]
        for i in range(size // HEAD):
            tile = slice(i * HEAD, (i + 1) * HEAD)
            q_ref[block, :, tile] = qa_ref[slot, tile, :]
            q_ref[block, :, size + i * HEAD : size + (i + 1) * HEAD] = qb_ref[slot, tile, :]

    def scores(step):
        block, begin, end, _ = step
        return lax.dot_general(k_ref[begin:end, :], q_ref[block], NN, preferred_element_type=F32)

    def run(steps, source):
        state = {}
        ahead = scores(steps[0])
        for at, (block, begin, end, masked) in enumerate(steps):
            s = ahead
            if at + 1 < len(steps):
                ahead = scores(steps[at + 1])
            if masked:
                shape = (s.shape[0], size)
                key_at = lax.broadcasted_iota(jnp.int32, shape, 0) + c * half
                allowed = key_at <= lax.broadcasted_iota(jnp.int32, shape, 1)
                s = jnp.where(jnp.concatenate([allowed, allowed], axis=1), s, NEG)
            if block not in state and source is not None:
                state[block] = tuple(ref[block] for ref in source)
            fresh = jnp.max(s, axis=0, keepdims=True)
            if block in state:
                m, l, a = state[block]
                fresh = jnp.maximum(m, fresh)
                shrink = jnp.exp2((m - fresh) * EXP_SCALE)
            weights = jnp.exp2(s * EXP_SCALE - fresh * EXP_SCALE)
            total = jnp.sum(weights, axis=0, keepdims=True)
            added = lax.dot_general(
                vt_ref[:, begin:end], weights.astype(BF16), NN, preferred_element_type=F32
            )
            if block in state:
                total, added = l * shrink + total, a * shrink + added
            state[block] = (fresh, total, added)
        for block, values in state.items():
            m_ref[block], l_ref[block], a_ref[block] = values

    def earlier(block):
        end = block * wide
        return [(block, at, min(at + 512, end), False) for at in range(0, end, 512)]

    def same(block, at):
        begin = block * wide + at * half
        return [(block, begin, begin + half, first)]

    if first:
        run(sum([earlier(block) + same(block, 0) for block in range(4)], []), None)
    else:
        for ref, out in zip(carried, (m_ref, l_ref, a_ref)):
            out[0] = ref[0]
        run(sum([earlier(block) for block in range(1, 4)], []), carried)
        for at in range(many):
            for odd in range(2):

                @pl.when(place_ref[2 + 2 * at + odd] > 0)
                def _():
                    run(same(odd, at) + same(odd + 2, at), (m_ref, l_ref, a_ref))

    if last:
        for head in range(2):
            lanes = slice(head * size, (head + 1) * size)
            for block in range(4):
                out = mine_out.at[block] if head == 0 else theirs_out[block // 2].at[block % 2]
                out[:HEAD, :] = a_ref[block, :, lanes]
                out[HEAD : HEAD + 1, :] = m_ref[block, :, lanes]
                out[HEAD + 1 : HEAD + 2, :] = l_ref[block, :, lanes]
                out[HEAD + 2 :, :] = jnp.zeros((6, size), F32)


def attend(first, last, place, queries, chunks, carry, after):
    many, size = len(chunks), queries[0].shape[1]
    state = [(4, 1, 2 * size), (4, 1, 2 * size), (4, HEAD, 2 * size)]
    keys = 4 * many * size // 2
    scratch = [pltpu.VMEM((keys, HEAD), BF16), pltpu.VMEM((HEAD, keys), BF16)]
    scratch.append(pltpu.VMEM((4, HEAD, 2 * size), BF16))
    if last:
        out_shape = [jax.ShapeDtypeStruct((many, HEAD + 8, size), F32) for many in (4, 2, 2)]
        scratch = [pltpu.VMEM(s, F32) for s in state] + scratch
    else:
        out_shape = [jax.ShapeDtypeStruct(s, F32) for s in state]
    carry = () if first else carry
    at = 3 + many

    def kernel(*refs):
        attend_kernel(first, last, many, len(after), *refs)

    return pl.pallas_call(
        kernel,
        out_shape=out_shape,
        in_specs=[SMEM] + [VMEM] * (2 + many + len(carry)) + [ANY] * len(after),
        out_specs=[VMEM] * len(out_shape),
        scratch_shapes=scratch,
        input_output_aliases={} if first or last else {at: 0, at + 1: 1, at + 2: 2},
        compiler_params=pltpu.CompilerParams(vmem_limit_bytes=LIMIT),
        cost_estimate=cost(4.5 * many),
        name="scorer_attend",
    )(place, *queries, *chunks, *carry, *after)


def merge_kernel(mine_ref, first_ref, second_ref, *refs):
    out_ref = refs[-1]
    for block in range(4):
        mine = mine_ref.at[block]
        got = (first_ref, second_ref)[block // 2].at[block % 2]
        m0, m1 = mine[HEAD : HEAD + 1, :], got[HEAD : HEAD + 1, :]
        top = jnp.maximum(m0, m1)
        f0, f1 = jnp.exp2((m0 - top) * EXP_SCALE), jnp.exp2((m1 - top) * EXP_SCALE)
        total = mine[HEAD + 1 : HEAD + 2, :] * f0 + got[HEAD + 1 : HEAD + 2, :] * f1
        mixed = mine[:HEAD, :] * f0 + got[:HEAD, :] * f1
        out_ref[block] = (mixed / total).T.astype(BF16)


def merge(mine, first, second, after):
    size = mine.shape[2]
    return pl.pallas_call(
        merge_kernel,
        out_shape=jax.ShapeDtypeStruct((4, size, HEAD), BF16),
        in_specs=[VMEM] * 3 + [ANY] * len(after),
        out_specs=VMEM,
        compiler_params=pltpu.CompilerParams(vmem_limit_bytes=LIMIT),
        cost_estimate=cost(1.5),
        name="merge",
    )(mine, first, second, *after)


def target_qkv_kernel(
    place_ref, b0, b1, b2, b3, gain_ref, qg_ref, kg_ref, cos_ref, sin_ref, wq_ref, wk_ref, wv_ref,
    *refs,
):
    q_out, kv_out, normed_ref, q_acc, k_acc, v_acc = refs[-6:]
    at = pl.program_id(0)
    steps = pl.num_programs(0)
    rows, part = b0.shape
    block = wq_ref.shape[0]

    @pl.when(at == 0)
    def _():
        blocks = in_order([b[...].astype(F32) for b in (b0, b1, b2, b3)], place_ref[0], place_ref[1])
        total = sum(jnp.sum(b * b, axis=-1, keepdims=True) for b in blocks)
        factor = lax.rsqrt(total / (4 * part) + EPS)
        for index in range(4):
            normed = blocks[index] * factor * gain_ref[:, index * part : (index + 1) * part]
            normed = normed.astype(BF16)
            for piece in range(part // block):
                normed_ref[index * (part // block) + piece] = normed[
                    :, piece * block : (piece + 1) * block
                ]
        q_acc[...] = jnp.zeros_like(q_acc)
        k_acc[...] = jnp.zeros_like(k_acc)
        v_acc[...] = jnp.zeros_like(v_acc)

    normed = normed_ref[at]
    q_acc[...] += lax.dot_general(normed, wq_ref[...], NN, preferred_element_type=F32)
    k_acc[...] += lax.dot_general(normed, wk_ref[...], NN, preferred_element_type=F32)
    v_acc[...] += lax.dot_general(normed, wv_ref[...], NN, preferred_element_type=F32)

    @pl.when(at == steps - 1)
    def _():
        cosine, sine = cos_ref[...], sin_ref[...]
        for h in range(8):
            turned = head_rope(q_acc[:, h * HEAD : (h + 1) * HEAD], qg_ref[...], cosine, sine)
            q_out[h // 4, (h % 4) * rows : (h % 4 + 1) * rows, :] = turned.astype(BF16)
        for h in range(2):
            lanes = slice(h * HEAD, (h + 1) * HEAD)
            turned = head_rope(k_acc[:, lanes], kg_ref[...], cosine, sine)
            kv_out[:, lanes] = turned.astype(BF16)
        kv_out[:, 2 * HEAD :] = v_acc[...].astype(BF16)


def target_qkv(place, blocks, gain, query_gain, key_gain, cosine, sine, wq, wk, wv, after):
    rows, part = blocks[0].shape
    block = 640
    steps = 4 * part // block
    whole = lambda shape: pl.BlockSpec(shape, lambda i: (0,) * len(shape))
    return pl.pallas_call(
        target_qkv_kernel,
        grid=(steps,),
        out_shape=[
            jax.ShapeDtypeStruct((2, 4 * rows, HEAD), BF16),
            jax.ShapeDtypeStruct((rows, 4 * HEAD), BF16),
        ],
        in_specs=[SMEM]
        + [whole((rows, part))] * 4
        + [whole(gain.shape), whole((1, HEAD)), whole((1, HEAD)), whole((rows, HEAD)), whole((rows, HEAD))]
        + [
            pl.BlockSpec((block, wq.shape[1]), lambda i: (i, 0)),
            pl.BlockSpec((block, wk.shape[1]), lambda i: (i, 0)),
            pl.BlockSpec((block, wv.shape[1]), lambda i: (i, 0)),
        ]
        + [ANY] * len(after),
        out_specs=[whole((2, 4 * rows, HEAD)), whole((rows, 4 * HEAD))],
        scratch_shapes=[
            pltpu.VMEM((steps, rows, block), BF16),
            pltpu.VMEM((rows, wq.shape[1]), F32),
            pltpu.VMEM((rows, wk.shape[1]), F32),
            pltpu.VMEM((rows, wv.shape[1]), F32),
        ],
        compiler_params=pltpu.CompilerParams(vmem_limit_bytes=LIMIT),
        cost_estimate=cost(6.5),
        name="target_qkv",
    )(place, *blocks, gain, query_gain, key_gain, cosine, sine, wq, wk, wv, *after)


def target_attend_kernel(place_ref, q_ref, c0, c1, c2, c3, after_ref, out_ref, m_ref, l_ref, a_ref):
    y, x, zh = place_ref[0], place_ref[1], place_ref[2]
    members = 4
    rows = q_ref.shape[1] // members

    def chunk(keys_ref, own):
        for g in range(2):
            keys = keys_ref[:, g * HEAD : (g + 1) * HEAD]
            values = keys_ref[:, (2 + g) * HEAD : (3 + g) * HEAD]
            s = lax.dot_general(q_ref[g], keys, NT, preferred_element_type=F32)
            if own:
                row = lax.broadcasted_iota(jnp.int32, (rows, s.shape[1]), 0) + (2 * x + zh) * rows
                key_at = lax.broadcasted_iota(jnp.int32, (rows, s.shape[1]), 1)
                allowed = jnp.concatenate([key_at <= row] * members, axis=0)
                s = jnp.where(allowed, s, NEG)
            fresh = jnp.max(s, axis=1, keepdims=True)
            if not own:
                m = m_ref[g]
                fresh = jnp.maximum(m, fresh)
                shrink = jnp.exp2((m - fresh) * EXP_SCALE)
            weights = jnp.exp2(s * EXP_SCALE - fresh * EXP_SCALE)
            total = jnp.sum(weights, axis=1, keepdims=True)
            added = lax.dot_general(weights.astype(BF16), values, NN, preferred_element_type=F32)
            if not own:
                total, added = l_ref[g] * shrink + total, a_ref[g] * shrink + added
            m_ref[g], l_ref[g], a_ref[g] = fresh, total, added

    chunk(c0, True)
    for by, ref in ((1, c1), (2, c2), (3, c3)):

        @pl.when(y >= by)
        def _():
            chunk(ref, False)

    for g in range(2):
        context = (a_ref[g] / l_ref[g]).astype(BF16)
        for member in range(members):
            lanes = slice((g * members + member) * HEAD, (g * members + member + 1) * HEAD)
            out_ref[:, lanes] = context[member * rows : (member + 1) * rows]


def target_attend(place, queries, chunks, after):
    groups, many, _ = queries.shape
    rows = many // 4
    return pl.pallas_call(
        target_attend_kernel,
        out_shape=jax.ShapeDtypeStruct((rows, 8 * HEAD), BF16),
        in_specs=[SMEM] + [VMEM] * 5 + [ANY],
        out_specs=VMEM,
        scratch_shapes=[
            pltpu.VMEM((groups, many, 1), F32),
            pltpu.VMEM((groups, many, 1), F32),
            pltpu.VMEM((groups, many, HEAD), F32),
        ],
        compiler_params=pltpu.CompilerParams(vmem_limit_bytes=LIMIT),
        cost_estimate=cost(6),
        name="target_attend",
    )(place, queries, *chunks, after)


def gather_tp(value, hops):
    chip = shift(value, "zl", 2, 1)
    if hops == 2:
        return [value, shift(value, "c", 2, 1), chip, shift(chip, "c", 2, 1)]
    away = [(i, i ^ 3) for i in range(4)]
    return [value, shift(value, "c", 2, 1), chip, lax.ppermute(value, TP, away)]


def exchange_y(blocks, y):
    got = [lax.dynamic_index_in_dim(blocks, y, 0, keepdims=False)]
    for by in (1, 2, 3):
        block = lax.dynamic_index_in_dim(blocks, lax.rem(y + by, 4), 0, keepdims=False)
        pairs = [
            (4 * i + j, (i + by) % 4 * 4 + (3 - j if by % 2 else j)) for i in range(4) for j in range(4)
        ]
        got.append(lax.ppermute(block, ("y", "x"), pairs))
    return got


def on_device(
    prompt_states,
    scorer_gain,
    scorer_query,
    scorer_key,
    scorer_value,
    scorer_querynorm,
    scorer_keynorm,
    scorer_project,
    target_embeds,
    target_gain,
    target_query,
    target_key,
    target_value,
    target_querynorm,
    target_keynorm,
    kept_rows,
    kept_counts,
    shard_order,
):
    y, x, zh, zl, c = (lax.axis_index(name) for name in ("y", "x", "zh", "zl", "c"))
    place = (y * 4 + x) * 2 + zh
    tp_place = jnp.stack([zl, c]).astype(jnp.int32)
    rows = prompt_states.shape[0]

    state_blocks = gather_tp(prompt_states, 1)
    weights = (scorer_query, scorer_key, scorer_value)
    got_weights = [
        shift(scorer_query, "c", 2, 1),
        shift(jnp.concatenate([scorer_key, scorer_value], axis=1), "c", 2, 1),
    ]
    got_project = shift(scorer_project, "c", 2, 1)
    cosine, sine = rope_tables(place * rows + jnp.arange(rows, dtype=jnp.int32))
    shards = shard_order.shape[0]
    features = target_embeds.shape[1]
    target_rows = kept_rows.shape[1] // 2
    counts = lax.all_to_all(jnp.broadcast_to(kept_counts[:, None], (shards, 1)), CTX, 0, 0, tiled=True)
    def exchange_rows(value):
        value = lax.all_to_all(value.reshape(shards, SLOTS, features), CTX, 0, 0, tiled=True)
        return value.reshape(shards * SLOTS, features)

    sent, select = route(
        place[None].astype(jnp.int32), counts, shard_order[:, None], kept_rows, target_embeds
    )
    mixed = scorer_qkv(
        tp_place, state_blocks, scorer_gain[None], *weights, *got_weights,
        scorer_querynorm[None], scorer_keynorm[None], cosine, sine, sent,
    )
    exchanged = exchange_y(mixed, y)
    placed = move(place_kernel, "place", shards * SLOTS, select, exchange_rows(sent), mixed)

    own, query = split(exchanged, placed)
    compressed = move(land_kernel, "land", target_rows, exchange_rows(placed), own)
    queries = (query, shift(query, "c", 2, 1))

    def chunk_from(by, flip):
        pairs = [
            (2 * i + j, (i + by) % 4 * 2 + (j + flip) % 2) for i in range(4) for j in range(2)
        ]
        return lax.ppermute(own, ("x", "zh"), pairs)

    def relations(by, flip):
        if by == 0:
            return [2 * zh - 1] * 2
        ahead = x - lax.rem(x - by + 4, 4)
        even = jnp.where(y % 2 == 0, ahead, -ahead)
        return [even, -even]

    def call(last, places, chunks, carry, after):
        scalars = jnp.stack([y, c] + sum([relations(*at) for at in places], [])).astype(jnp.int32)
        return attend(carry is None, last, scalars, queries, chunks, carry, after)

    near = [(0, 1), (1, 0), (3, 0), (2, 0)]
    far = [(1, 1), (3, 1), (2, 1)]
    near_chunks = [chunk_from(*at) for at in near]
    far_chunks = [shift(near_chunks[0], "x", 4, at[0]) for at in far]
    carry = call(False, [], [own], None, [compressed, got_project])

    target_cos, target_sin = rope_tables(place * target_rows + jnp.arange(target_rows, dtype=jnp.int32))
    target_queries, target_kv = target_qkv(
        tp_place, gather_tp(compressed, 2), target_gain[None], target_querynorm[None], target_keynorm[None],
        target_cos, target_sin, target_query, target_key, target_value, [],
    )
    carry = call(False, near, near_chunks, carry, [target_kv])

    line = lax.all_to_all(
        jnp.broadcast_to(target_kv, (8, *target_kv.shape)), ("x", "zh"), 0, 0, tiled=True
    ).reshape(8 * target_rows, -1)
    mine, *theirs = call(True, far, far_chunks, carry, [line])
    chunks = [line] + [
        lax.ppermute(line, "y", [(i, i + by) for i in range(4 - by)]) for by in (1, 2, 3)
    ]
    attended = merge(mine, *(shift(half, "c", 2, 1) for half in theirs), chunks[1:])

    away, home = project(
        jnp.stack([y, c]).astype(jnp.int32), exchange_y(attended, y), scorer_project, got_project, []
    )
    summed = home + shift(away, "c", 2, 1).astype(F32)
    leaving = lax.dynamic_index_in_dim(summed, 1 - zl, 0, keepdims=False).astype(BF16)
    staying = lax.dynamic_index_in_dim(summed, zl, 0, keepdims=False)
    scorer_states = (staying + shift(leaving, "zl", 2, 1).astype(F32)).astype(BF16)

    target_place = jnp.stack([y, x, zh]).astype(jnp.int32)
    target_context = target_attend(target_place, target_queries, chunks, away)
    return (scorer_states, target_context)


def solution(mesh):
    fine = Mesh(mesh.devices.reshape(4, 4, 2, 2, 2), CTX + TP)
    return jax.shard_map(
        on_device,
        mesh=fine,
        in_specs=(
            P(CTX, TP),
            P(),
            P(None, TP),
            P(None, TP),
            P(None, TP),
            P(),
            P(),
            P(TP, None),
            P(CTX, TP),
            P(),
            P(None, TP),
            P(None, TP),
            P(None, TP),
            P(),
            P(),
            P(CTX, None),
            P(CTX),
            P(),
        ),
        out_specs=(P(CTX, TP), P(CTX, TP)),
        check_vma=False,
    )
```

```python
import jax
import jax.numpy as jnp
import numpy as np
from jax import lax
from jax.experimental import pallas as pl
from jax.experimental.pallas import tpu as pltpu
from jax.sharding import Mesh
from jax.sharding import PartitionSpec as P

F32 = jnp.float32
BF16 = jnp.bfloat16
EPS = 1e-06
ROPE_BASE = 1000000.0
NEG = -1e30
HEAD = 128
EXP_SCALE = float(HEAD**-0.5 * np.log2(np.e))
CTX = ("y", "x", "zh")
TP = ("zl", "c")
VMEM = pl.BlockSpec(memory_space=pltpu.VMEM)
SMEM = pl.BlockSpec(memory_space=pltpu.SMEM)
ANY = pl.BlockSpec(memory_space=pl.ANY)
LIMIT = 24 << 20
SCALE = 0.25


def cost(microseconds):
    return pl.CostEstimate(
        flops=int(microseconds * SCALE * 1.1e9), bytes_accessed=1024, transcendentals=0
    )
NN = (((1,), (0,)), ((), ()))
NT = (((1,), (1,)), ((), ()))


def shift(value, axis, size, by):
    return lax.ppermute(value, axis, [(i, (i + by) % size) for i in range(size)])


def rope_tables(positions):
    lane = jnp.arange(HEAD)
    freqs = ROPE_BASE ** ((lane % (HEAD // 2)).astype(F32) * (-2.0 / HEAD))
    angles = positions.astype(F32)[:, None] * freqs[None, :]
    return jnp.cos(angles), jnp.where(lane < HEAD // 2, -1.0, 1.0)[None, :] * jnp.sin(angles)


def head_rope(values, gain, cosine, sine):
    mean_square = jnp.mean(values * values, axis=-1, keepdims=True)
    normed = values * lax.rsqrt(mean_square + EPS) * gain
    return normed * cosine + pltpu.roll(normed, HEAD // 2, 1) * sine


def in_order(blocks, zl, c):
    b0, b1, b2, b3 = blocks
    first, second = jnp.where(c == 0, b0, b1), jnp.where(c == 0, b1, b0)
    third, fourth = jnp.where(c == 0, b2, b3), jnp.where(c == 0, b3, b2)
    low, high = zl == 0, zl != 0
    return (
        jnp.where(low, first, third),
        jnp.where(low, second, fourth),
        jnp.where(high, first, third),
        jnp.where(high, second, fourth),
    )


def scorer_qkv_kernel(
    place_ref, b0, b1, b2, b3, gain_ref, wq_ref, wk_ref, wv_ref, gq_ref, gkv_ref,
    qg_ref, kg_ref, cos_ref, sin_ref, after_ref, out_ref, w_ref, normed_ref,
):
    zl, c = place_ref[0], place_ref[1]
    pair = 2 * HEAD
    for i in range(2):
        mine, got = (
            jnp.where(
                c == 0,
                ref[:, 2 * i * HEAD : (2 * i + 1) * HEAD],
                ref[:, (2 * i + 1) * HEAD : (2 * i + 2) * HEAD],
            )
            for ref in (wq_ref, gq_ref)
        )
        w_ref[:, i * HEAD : (i + 1) * HEAD] = jnp.where(c == 0, mine, got)
        w_ref[:, pair + i * HEAD : pair + (i + 1) * HEAD] = jnp.where(c == 0, got, mine)
    for i, own_ref in ((1, wk_ref), (2, wv_ref)):
        own, got = own_ref[...], gkv_ref[:, (i - 1) * pair : i * pair]
        w_ref[:, 2 * i * pair : (2 * i + 1) * pair] = jnp.where(c == 0, own, got)
        w_ref[:, (2 * i + 1) * pair : (2 * i + 2) * pair] = jnp.where(c == 0, got, own)
    step, many = 128, b0.shape[0]
    half = many // 2
    for part in range(many // step):
        rows = slice(part * step, (part + 1) * step)
        blocks = in_order([b[rows, :].astype(F32) for b in (b0, b1, b2, b3)], zl, c)
        states = jnp.concatenate(blocks, axis=1)
        mean_square = jnp.mean(states * states, axis=-1, keepdims=True)
        normed = (states * lax.rsqrt(mean_square + EPS) * gain_ref[...]).astype(BF16)
        normed_ref[rows, :] = normed
        mixed = lax.dot_general(normed, w_ref[:, : 2 * pair], NN, preferred_element_type=F32)
        for h in range(4):
            turned = head_rope(
                mixed[:, h * HEAD : (h + 1) * HEAD], qg_ref[...], cos_ref[rows, :], sin_ref[rows, :]
            )
            out_ref[h, many + part * step : many + (part + 1) * step, :] = turned.T.astype(BF16)
    for part in range(half // step):
        rows = pl.ds(pl.multiple_of(c * half + part * step, step), step)
        mixed = lax.dot_general(
            normed_ref[rows, :], w_ref[:, 2 * pair :], NN, preferred_element_type=F32
        )
        for h in range(4):
            key = head_rope(
                mixed[:, h * HEAD : (h + 1) * HEAD], kg_ref[...], cos_ref[rows, :], sin_ref[rows, :]
            )
            out_ref[h, part * step : (part + 1) * step, :] = key.astype(BF16)
            value = mixed[:, (4 + h) * HEAD : (5 + h) * HEAD].T
            out_ref[h, half + part * step : half + (part + 1) * step, :] = value.astype(BF16)


def scorer_qkv(place, blocks, *rest):
    rows = blocks[0].shape[0]
    return pl.pallas_call(
        scorer_qkv_kernel,
        out_shape=jax.ShapeDtypeStruct((4, 2 * rows, HEAD), BF16),
        in_specs=[SMEM] + [VMEM] * (3 + len(rest)) + [ANY],
        out_specs=VMEM,
        scratch_shapes=[
            pltpu.VMEM((4 * blocks[0].shape[1], 12 * HEAD), BF16),
            pltpu.VMEM((rows, 4 * blocks[0].shape[1]), BF16),
        ],
        compiler_params=pltpu.CompilerParams(vmem_limit_bytes=LIMIT),
        cost_estimate=cost(7),
        name="scorer_qkv",
    )(place, *blocks, *rest)


def project_kernel(place_ref, a0, a1, a2, a3, w_ref, got_ref, *refs):
    away_out, home_out, pick_ref = refs[-3:]
    y, c = place_ref[0], place_ref[1]
    heads = [None] * 4
    for i in range(2):
        mine, got = (
            jnp.where(
                c == 0,
                ref[2 * i * HEAD : (2 * i + 1) * HEAD, :],
                ref[(2 * i + 1) * HEAD : (2 * i + 2) * HEAD, :],
            )
            for ref in (w_ref, got_ref)
        )
        heads[i] = jnp.where(c == 0, mine, got)
        heads[2 + i] = jnp.where(c == 0, got, mine)
    width = w_ref.shape[1] // 4
    for at in range(4):
        slot = lax.rem(y - at + 4, 4)
        for block in range(4):
            pick_ref[block, pl.ds(pl.multiple_of(slot * HEAD, HEAD), HEAD), :] = heads[at][
                :, block * width : (block + 1) * width
            ]
    attended = jnp.concatenate([a[...] for a in (a0, a1, a2, a3)], axis=1)
    for zl in range(2):
        away_out[zl] = lax.dot_general(
            attended, pick_ref[zl * 2 + 1 - c], NN, preferred_element_type=F32
        ).astype(BF16)
        home_out[zl] = lax.dot_general(attended, pick_ref[zl * 2 + c], NN, preferred_element_type=F32)


def project(place, attended, weight, got, after):
    rows, width = attended[0].shape[0], weight.shape[1] // 4
    return pl.pallas_call(
        project_kernel,
        out_shape=[
            jax.ShapeDtypeStruct((2, rows, width), BF16),
            jax.ShapeDtypeStruct((2, rows, width), F32),
        ],
        in_specs=[SMEM] + [VMEM] * 6 + [ANY] * len(after),
        out_specs=[VMEM] * 2,
        scratch_shapes=[pltpu.VMEM((4, 4 * HEAD, width), BF16)],
        compiler_params=pltpu.CompilerParams(vmem_limit_bytes=LIMIT),
        cost_estimate=cost(2.5),
        name="scorer_project",
    )(place, *attended, weight, got, *after)


SLOTS = 8


def route_kernel(place_ref, counts_ref, order_ref, rows_ref, embeds_ref, sent_out, select_out):
    place = place_ref[0]
    shards, capacity = counts_ref.shape[0], rows_ref.shape[1]
    turns, entries = capacity // shards, sent_out.shape[0]
    iota = lambda shape, axis: lax.broadcasted_iota(jnp.int32, shape, axis)
    square = (shards, shards)
    counts = counts_ref[...]
    eye = iota(square, 0) == iota(square, 1)
    rank_row = jnp.sum(
        jnp.where(order_ref[...] == iota(square, 1), iota(square, 0), 0), axis=0, keepdims=True
    )
    rank = jnp.sum(jnp.where(eye, rank_row, 0), axis=1, keepdims=True)
    count_row = jnp.sum(jnp.where(eye, counts, 0), axis=0, keepdims=True)
    starts = jnp.sum(jnp.where(rank_row < rank, count_row, 0), axis=1, keepdims=True)
    my_start = jnp.sum(jnp.where(iota((shards, 1), 0) == place, starts, 0))
    entry = iota((entries, 1), 0)
    slot = ((entry // SLOTS - my_start) & (shards - 1)) + shards * (entry % SLOTS)
    picked = jnp.sum(
        jnp.where(iota((entries, capacity), 1) == slot, rows_ref[...], 0), axis=1, keepdims=True
    )
    pick = jnp.where(iota((entries, embeds_ref.shape[0]), 1) == picked, 1.0, 0.0).astype(BF16)
    sent_out[...] = lax.dot_general(
        pick, embeds_ref[...], NN, preferred_element_type=F32
    ).astype(BF16)
    wide = (shards, entries)
    source = iota(wide, 0) == iota(wide, 1) // SLOTS
    start = jnp.sum(jnp.where(source, starts, 0), axis=0, keepdims=True)
    count = jnp.sum(jnp.where(source, counts, 0), axis=0, keepdims=True)
    turn = iota((1, entries), 1) % SLOTS
    within = ((place - start) & (shards - 1)) + shards * turn
    good = (within < count) & (turn < turns)
    turn_at = (start + within) // shards
    dest = jnp.where(good, turn_at // 3 * SLOTS + turn_at % 3, -1)
    select_out[...] = jnp.where(iota(select_out.shape, 0) == dest, 1.0, 0.0).astype(BF16)


def route(place, counts, order, rows, embeds):
    entries = rows.shape[0] * counts.shape[0] * SLOTS
    return pl.pallas_call(
        route_kernel,
        out_shape=[
            jax.ShapeDtypeStruct((entries, embeds.shape[1]), BF16),
            jax.ShapeDtypeStruct((entries, entries), BF16),
        ],
        in_specs=[SMEM] + [VMEM] * 4,
        out_specs=[VMEM] * 2,
        compiler_params=pltpu.CompilerParams(vmem_limit_bytes=LIMIT),
        cost_estimate=cost(1),
        name="route",
    )(place, counts, order, rows, embeds)


def place_kernel(select_ref, rows_ref, after_ref, out_ref):
    out_ref[...] = lax.dot_general(
        select_ref[...], rows_ref[...], NN, preferred_element_type=F32
    ).astype(BF16)


def land_kernel(rows_ref, after_ref, out_ref):
    shape = (out_ref.shape[0], rows_ref.shape[0])
    shards = shape[1] // SLOTS
    row, entry = lax.broadcasted_iota(jnp.int32, shape, 0), lax.broadcasted_iota(jnp.int32, shape, 1)
    wanted = (row % shards) * SLOTS + row // shards
    select = jnp.where(entry == wanted, 1.0, 0.0).astype(BF16)
    out_ref[...] = lax.dot_general(
        select, rows_ref[...], NN, preferred_element_type=F32
    ).astype(BF16)


def move(kernel, name, rows, *operands):
    return pl.pallas_call(
        kernel,
        out_shape=jax.ShapeDtypeStruct((rows, operands[-2].shape[1]), BF16),
        in_specs=[VMEM] * (len(operands) - 1) + [ANY],
        out_specs=VMEM,
        compiler_params=pltpu.CompilerParams(vmem_limit_bytes=LIMIT),
        cost_estimate=cost(0.5),
        name=name,
    )(*operands)


def split_kernel(b0, b1, b2, b3, after_ref, own_out, query_out):
    size = own_out.shape[1]
    for at, ref in enumerate((b0, b1, b2, b3)):
        own_out[at] = ref[:size, :]
        query_out[at] = ref[size:, :]


def split(blocks, after):
    size = blocks[0].shape[0] // 2
    return pl.pallas_call(
        split_kernel,
        out_shape=[jax.ShapeDtypeStruct((4, size, HEAD), BF16)] * 2,
        in_specs=[VMEM] * 4 + [ANY],
        out_specs=[VMEM] * 2,
        cost_estimate=cost(40),
        name="split",
    )(*blocks, after)


def attend_kernel(first, last, many, waits, *refs):
    place_ref, qa_ref, qb_ref = refs[:3]
    chunk_refs, refs = refs[3 : 3 + many], refs[3 + many :]
    carried = None
    if not first:
        carried, refs = refs[:3], refs[3:]
    refs = refs[waits:]
    if last:
        mine_out, *theirs_out = refs[:3]
        refs = refs[3:]
    m_ref, l_ref, a_ref, k_ref, vt_ref, q_ref = refs
    y, c = place_ref[0], place_ref[1]
    size = qa_ref.shape[1]
    half = size // 2
    wide = half * many
    for block in range(4):
        slot = lax.rem(y - block + 4, 4)
        for at, ref in enumerate(chunk_refs):
            chunk = ref[slot]
            k_ref[(block * many + at) * half : (block * many + at + 1) * half, :] = chunk[:half]
            for i in range(half // HEAD):
                lanes = (block * many + at) * half + i * HEAD
                vt_ref[:, lanes : lanes + HEAD] = chunk[half + i * HEAD : half + (i + 1) * HEAD]
        for i in range(size // HEAD):
            tile = slice(i * HEAD, (i + 1) * HEAD)
            q_ref[block, :, tile] = qa_ref[slot, tile, :]
            q_ref[block, :, size + i * HEAD : size + (i + 1) * HEAD] = qb_ref[slot, tile, :]

    def scores(step):
        block, begin, end, _ = step
        return lax.dot_general(k_ref[begin:end, :], q_ref[block], NN, preferred_element_type=F32)

    def run(steps, source):
        state = {}
        ahead = scores(steps[0])
        for at, (block, begin, end, masked) in enumerate(steps):
            s = ahead
            if at + 1 < len(steps):
                ahead = scores(steps[at + 1])
            if masked:
                shape = (s.shape[0], size)
                key_at = lax.broadcasted_iota(jnp.int32, shape, 0) + c * half
                allowed = key_at <= lax.broadcasted_iota(jnp.int32, shape, 1)
                s = jnp.where(jnp.concatenate([allowed, allowed], axis=1), s, NEG)
            if block not in state and source is not None:
                state[block] = tuple(ref[block] for ref in source)
            fresh = jnp.max(s, axis=0, keepdims=True)
            if block in state:
                m, l, a = state[block]
                fresh = jnp.maximum(m, fresh)
                shrink = jnp.exp2((m - fresh) * EXP_SCALE)
            weights = jnp.exp2(s * EXP_SCALE - fresh * EXP_SCALE)
            total = jnp.sum(weights, axis=0, keepdims=True)
            added = lax.dot_general(
                vt_ref[:, begin:end], weights.astype(BF16), NN, preferred_element_type=F32
            )
            if block in state:
                total, added = l * shrink + total, a * shrink + added
            state[block] = (fresh, total, added)
        for block, values in state.items():
            m_ref[block], l_ref[block], a_ref[block] = values

    def earlier(block):
        end = block * wide
        return [(block, at, min(at + 512, end), False) for at in range(0, end, 512)]

    def same(block, at):
        begin = block * wide + at * half
        return [(block, begin, begin + half, first)]

    if first:
        run(sum([earlier(block) + same(block, 0) for block in range(4)], []), None)
    else:
        for ref, out in zip(carried, (m_ref, l_ref, a_ref)):
            out[0] = ref[0]
        run(sum([earlier(block) for block in range(1, 4)], []), carried)
        for at in range(many):
            for odd in range(2):

                @pl.when(place_ref[2 + 2 * at + odd] > 0)
                def _():
                    run(same(odd, at) + same(odd + 2, at), (m_ref, l_ref, a_ref))

    if last:
        for head in range(2):
            lanes = slice(head * size, (head + 1) * size)
            for block in range(4):
                out = mine_out.at[block] if head == 0 else theirs_out[block // 2].at[block % 2]
                out[:HEAD, :] = a_ref[block, :, lanes]
                out[HEAD : HEAD + 1, :] = m_ref[block, :, lanes]
                out[HEAD + 1 : HEAD + 2, :] = l_ref[block, :, lanes]
                out[HEAD + 2 :, :] = jnp.zeros((6, size), F32)


def attend(first, last, place, queries, chunks, carry, after):
    many, size = len(chunks), queries[0].shape[1]
    state = [(4, 1, 2 * size), (4, 1, 2 * size), (4, HEAD, 2 * size)]
    keys = 4 * many * size // 2
    scratch = [pltpu.VMEM((keys, HEAD), BF16), pltpu.VMEM((HEAD, keys), BF16)]
    scratch.append(pltpu.VMEM((4, HEAD, 2 * size), BF16))
    if last:
        out_shape = [jax.ShapeDtypeStruct((many, HEAD + 8, size), F32) for many in (4, 2, 2)]
        scratch = [pltpu.VMEM(s, F32) for s in state] + scratch
    else:
        out_shape = [jax.ShapeDtypeStruct(s, F32) for s in state]
    carry = () if first else carry
    at = 3 + many

    def kernel(*refs):
        attend_kernel(first, last, many, len(after), *refs)

    return pl.pallas_call(
        kernel,
        out_shape=out_shape,
        in_specs=[SMEM] + [VMEM] * (2 + many + len(carry)) + [ANY] * len(after),
        out_specs=[VMEM] * len(out_shape),
        scratch_shapes=scratch,
        input_output_aliases={} if first or last else {at: 0, at + 1: 1, at + 2: 2},
        compiler_params=pltpu.CompilerParams(vmem_limit_bytes=LIMIT),
        cost_estimate=cost(4.5 * many),
        name="scorer_attend",
    )(place, *queries, *chunks, *carry, *after)


def merge_kernel(mine_ref, first_ref, second_ref, *refs):
    out_ref = refs[-1]
    for block in range(4):
        mine = mine_ref.at[block]
        got = (first_ref, second_ref)[block // 2].at[block % 2]
        m0, m1 = mine[HEAD : HEAD + 1, :], got[HEAD : HEAD + 1, :]
        top = jnp.maximum(m0, m1)
        f0, f1 = jnp.exp2((m0 - top) * EXP_SCALE), jnp.exp2((m1 - top) * EXP_SCALE)
        total = mine[HEAD + 1 : HEAD + 2, :] * f0 + got[HEAD + 1 : HEAD + 2, :] * f1
        mixed = mine[:HEAD, :] * f0 + got[:HEAD, :] * f1
        out_ref[block] = (mixed / total).T.astype(BF16)


def merge(mine, first, second, after):
    size = mine.shape[2]
    return pl.pallas_call(
        merge_kernel,
        out_shape=jax.ShapeDtypeStruct((4, size, HEAD), BF16),
        in_specs=[VMEM] * 3 + [ANY] * len(after),
        out_specs=VMEM,
        compiler_params=pltpu.CompilerParams(vmem_limit_bytes=LIMIT),
        cost_estimate=cost(1.5),
        name="merge",
    )(mine, first, second, *after)


def target_qkv_kernel(
    place_ref, b0, b1, b2, b3, gain_ref, qg_ref, kg_ref, cos_ref, sin_ref, wq_ref, wk_ref, wv_ref,
    *refs,
):
    q_out, kv_out, normed_ref, q_acc, k_acc, v_acc = refs[-6:]
    at = pl.program_id(0)
    steps = pl.num_programs(0)
    rows, part = b0.shape
    block = wq_ref.shape[0]

    @pl.when(at == 0)
    def _():
        blocks = in_order([b[...].astype(F32) for b in (b0, b1, b2, b3)], place_ref[0], place_ref[1])
        total = sum(jnp.sum(b * b, axis=-1, keepdims=True) for b in blocks)
        factor = lax.rsqrt(total / (4 * part) + EPS)
        for index in range(4):
            normed = blocks[index] * factor * gain_ref[:, index * part : (index + 1) * part]
            normed = normed.astype(BF16)
            for piece in range(part // block):
                normed_ref[index * (part // block) + piece] = normed[
                    :, piece * block : (piece + 1) * block
                ]
        q_acc[...] = jnp.zeros_like(q_acc)
        k_acc[...] = jnp.zeros_like(k_acc)
        v_acc[...] = jnp.zeros_like(v_acc)

    normed = normed_ref[at]
    q_acc[...] += lax.dot_general(normed, wq_ref[...], NN, preferred_element_type=F32)
    k_acc[...] += lax.dot_general(normed, wk_ref[...], NN, preferred_element_type=F32)
    v_acc[...] += lax.dot_general(normed, wv_ref[...], NN, preferred_element_type=F32)

    @pl.when(at == steps - 1)
    def _():
        cosine, sine = cos_ref[...], sin_ref[...]
        for h in range(8):
            turned = head_rope(q_acc[:, h * HEAD : (h + 1) * HEAD], qg_ref[...], cosine, sine)
            q_out[h // 4, (h % 4) * rows : (h % 4 + 1) * rows, :] = turned.astype(BF16)
        for h in range(2):
            lanes = slice(h * HEAD, (h + 1) * HEAD)
            turned = head_rope(k_acc[:, lanes], kg_ref[...], cosine, sine)
            kv_out[:, lanes] = turned.astype(BF16)
        kv_out[:, 2 * HEAD :] = v_acc[...].astype(BF16)


def target_qkv(place, blocks, gain, query_gain, key_gain, cosine, sine, wq, wk, wv, after):
    rows, part = blocks[0].shape
    block = 640
    steps = 4 * part // block
    whole = lambda shape: pl.BlockSpec(shape, lambda i: (0,) * len(shape))
    return pl.pallas_call(
        target_qkv_kernel,
        grid=(steps,),
        out_shape=[
            jax.ShapeDtypeStruct((2, 4 * rows, HEAD), BF16),
            jax.ShapeDtypeStruct((rows, 4 * HEAD), BF16),
        ],
        in_specs=[SMEM]
        + [whole((rows, part))] * 4
        + [whole(gain.shape), whole((1, HEAD)), whole((1, HEAD)), whole((rows, HEAD)), whole((rows, HEAD))]
        + [
            pl.BlockSpec((block, wq.shape[1]), lambda i: (i, 0)),
            pl.BlockSpec((block, wk.shape[1]), lambda i: (i, 0)),
            pl.BlockSpec((block, wv.shape[1]), lambda i: (i, 0)),
        ]
        + [ANY] * len(after),
        out_specs=[whole((2, 4 * rows, HEAD)), whole((rows, 4 * HEAD))],
        scratch_shapes=[
            pltpu.VMEM((steps, rows, block), BF16),
            pltpu.VMEM((rows, wq.shape[1]), F32),
            pltpu.VMEM((rows, wk.shape[1]), F32),
            pltpu.VMEM((rows, wv.shape[1]), F32),
        ],
        compiler_params=pltpu.CompilerParams(vmem_limit_bytes=LIMIT),
        cost_estimate=cost(6.5),
        name="target_qkv",
    )(place, *blocks, gain, query_gain, key_gain, cosine, sine, wq, wk, wv, *after)


def target_attend_kernel(place_ref, q_ref, c0, c1, c2, c3, after_ref, out_ref, m_ref, l_ref, a_ref):
    y, x, zh = place_ref[0], place_ref[1], place_ref[2]
    members = 4
    rows = q_ref.shape[1] // members

    def chunk(keys_ref, own):
        for g in range(2):
            keys = keys_ref[:, g * HEAD : (g + 1) * HEAD]
            values = keys_ref[:, (2 + g) * HEAD : (3 + g) * HEAD]
            s = lax.dot_general(q_ref[g], keys, NT, preferred_element_type=F32)
            if own:
                row = lax.broadcasted_iota(jnp.int32, (rows, s.shape[1]), 0) + (2 * x + zh) * rows
                key_at = lax.broadcasted_iota(jnp.int32, (rows, s.shape[1]), 1)
                allowed = jnp.concatenate([key_at <= row] * members, axis=0)
                s = jnp.where(allowed, s, NEG)
            fresh = jnp.max(s, axis=1, keepdims=True)
            if not own:
                m = m_ref[g]
                fresh = jnp.maximum(m, fresh)
                shrink = jnp.exp2((m - fresh) * EXP_SCALE)
            weights = jnp.exp2(s * EXP_SCALE - fresh * EXP_SCALE)
            total = jnp.sum(weights, axis=1, keepdims=True)
            added = lax.dot_general(weights.astype(BF16), values, NN, preferred_element_type=F32)
            if not own:
                total, added = l_ref[g] * shrink + total, a_ref[g] * shrink + added
            m_ref[g], l_ref[g], a_ref[g] = fresh, total, added

    chunk(c0, True)
    for by, ref in ((1, c1), (2, c2), (3, c3)):

        @pl.when(y >= by)
        def _():
            chunk(ref, False)

    for g in range(2):
        context = (a_ref[g] / l_ref[g]).astype(BF16)
        for member in range(members):
            lanes = slice((g * members + member) * HEAD, (g * members + member + 1) * HEAD)
            out_ref[:, lanes] = context[member * rows : (member + 1) * rows]


def target_attend(place, queries, chunks, after):
    groups, many, _ = queries.shape
    rows = many // 4
    return pl.pallas_call(
        target_attend_kernel,
        out_shape=jax.ShapeDtypeStruct((rows, 8 * HEAD), BF16),
        in_specs=[SMEM] + [VMEM] * 5 + [ANY],
        out_specs=VMEM,
        scratch_shapes=[
            pltpu.VMEM((groups, many, 1), F32),
            pltpu.VMEM((groups, many, 1), F32),
            pltpu.VMEM((groups, many, HEAD), F32),
        ],
        compiler_params=pltpu.CompilerParams(vmem_limit_bytes=LIMIT),
        cost_estimate=cost(6),
        name="target_attend",
    )(place, queries, *chunks, after)


def gather_tp(value, hops):
    chip = shift(value, "zl", 2, 1)
    if hops == 2:
        return [value, shift(value, "c", 2, 1), chip, shift(chip, "c", 2, 1)]
    away = [(i, i ^ 3) for i in range(4)]
    return [value, shift(value, "c", 2, 1), chip, lax.ppermute(value, TP, away)]


def exchange_y(blocks, y):
    got = [lax.dynamic_index_in_dim(blocks, y, 0, keepdims=False)]
    for by in (1, 2, 3):
        block = lax.dynamic_index_in_dim(blocks, lax.rem(y + by, 4), 0, keepdims=False)
        pairs = [
            (4 * i + j, (i + by) % 4 * 4 + (3 - j if by % 2 else j)) for i in range(4) for j in range(4)
        ]
        got.append(lax.ppermute(block, ("y", "x"), pairs))
    return got


def on_device(
    prompt_states,
    scorer_gain,
    scorer_query,
    scorer_key,
    scorer_value,
    scorer_querynorm,
    scorer_keynorm,
    scorer_project,
    target_embeds,
    target_gain,
    target_query,
    target_key,
    target_value,
    target_querynorm,
    target_keynorm,
    kept_rows,
    kept_counts,
    shard_order,
):
    y, x, zh, zl, c = (lax.axis_index(name) for name in ("y", "x", "zh", "zl", "c"))
    place = (y * 4 + x) * 2 + zh
    tp_place = jnp.stack([zl, c]).astype(jnp.int32)
    rows = prompt_states.shape[0]

    state_blocks = gather_tp(prompt_states, 1)
    weights = (scorer_query, scorer_key, scorer_value)
    got_weights = [
        shift(scorer_query, "c", 2, 1),
        shift(jnp.concatenate([scorer_key, scorer_value], axis=1), "c", 2, 1),
    ]
    got_project = shift(scorer_project, "c", 2, 1)
    cosine, sine = rope_tables(place * rows + jnp.arange(rows, dtype=jnp.int32))
    shards = shard_order.shape[0]
    features = target_embeds.shape[1]
    target_rows = kept_rows.shape[1] // 2
    counts = lax.all_to_all(jnp.broadcast_to(kept_counts[:, None], (shards, 1)), CTX, 0, 0, tiled=True)
    def exchange_rows(value):
        value = lax.all_to_all(value.reshape(shards, SLOTS, features), CTX, 0, 0, tiled=True)
        return value.reshape(shards * SLOTS, features)

    sent, select = route(
        place[None].astype(jnp.int32), counts, shard_order[:, None], kept_rows, target_embeds
    )
    mixed = scorer_qkv(
        tp_place, state_blocks, scorer_gain[None], *weights, *got_weights,
        scorer_querynorm[None], scorer_keynorm[None], cosine, sine, sent,
    )
    exchanged = exchange_y(mixed, y)
    placed = move(place_kernel, "place", shards * SLOTS, select, exchange_rows(sent), mixed)

    own, query = split(exchanged, placed)
    compressed = move(land_kernel, "land", target_rows, exchange_rows(placed), own)
    queries = (query, shift(query, "c", 2, 1))

    def chunk_from(by, flip):
        pairs = [
            (2 * i + j, (i + by) % 4 * 2 + (j + flip) % 2) for i in range(4) for j in range(2)
        ]
        return lax.ppermute(own, ("x", "zh"), pairs)

    def relations(by, flip):
        if by == 0:
            return [2 * zh - 1] * 2
        ahead = x - lax.rem(x - by + 4, 4)
        even = jnp.where(y % 2 == 0, ahead, -ahead)
        return [even, -even]

    def call(last, places, chunks, carry, after):
        scalars = jnp.stack([y, c] + sum([relations(*at) for at in places], [])).astype(jnp.int32)
        return attend(carry is None, last, scalars, queries, chunks, carry, after)

    near = [(0, 1), (1, 0), (3, 0), (2, 0)]
    far = [(1, 1), (3, 1), (2, 1)]
    near_chunks = [chunk_from(*at) for at in near]
    far_chunks = [shift(near_chunks[0], "x", 4, at[0]) for at in far]
    carry = call(False, [], [own], None, [compressed, got_project])

    target_cos, target_sin = rope_tables(place * target_rows + jnp.arange(target_rows, dtype=jnp.int32))
    target_queries, target_kv = target_qkv(
        tp_place, gather_tp(compressed, 2), target_gain[None], target_querynorm[None], target_keynorm[None],
        target_cos, target_sin, target_query, target_key, target_value, [],
    )
    carry = call(False, near, near_chunks, carry, [target_kv])

    line = lax.all_to_all(
        jnp.broadcast_to(target_kv, (8, *target_kv.shape)), ("x", "zh"), 0, 0, tiled=True
    ).reshape(8 * target_rows, -1)
    mine, *theirs = call(True, far, far_chunks, carry, [line])
    chunks = [line] + [
        lax.ppermute(line, "y", [(i, i + by) for i in range(4 - by)]) for by in (1, 2, 3)
    ]
    attended = merge(mine, *(shift(half, "c", 2, 1) for half in theirs), chunks[1:])

    away, home = project(
        jnp.stack([y, c]).astype(jnp.int32), exchange_y(attended, y), scorer_project, got_project, []
    )
    summed = home + shift(away, "c", 2, 1).astype(F32)
    leaving = lax.dynamic_index_in_dim(summed, 1 - zl, 0, keepdims=False).astype(BF16)
    staying = lax.dynamic_index_in_dim(summed, zl, 0, keepdims=False)
    scorer_states = (staying + shift(leaving, "zl", 2, 1).astype(F32)).astype(BF16)

    target_place = jnp.stack([y, x, zh]).astype(jnp.int32)
    target_context = target_attend(target_place, target_queries, chunks, away)
    return (scorer_states, target_context)


def solution(mesh):
    fine = Mesh(mesh.devices.reshape(4, 4, 2, 2, 2), CTX + TP)
    return jax.shard_map(
        on_device,
        mesh=fine,
        in_specs=(
            P(CTX, TP),
            P(),
            P(None, TP),
            P(None, TP),
            P(None, TP),
            P(),
            P(),
            P(TP, None),
            P(CTX, TP),
            P(),
            P(None, TP),
            P(None, TP),
            P(None, TP),
            P(),
            P(),
            P(CTX, None),
            P(CTX),
            P(),
        ),
        out_specs=(P(CTX, TP), P(CTX, TP)),
        check_vma=False,
    )
```

```python
import jax
import jax.numpy as jnp
import numpy as np
from jax import lax
from jax.experimental import pallas as pl
from jax.experimental.pallas import tpu as pltpu
from jax.sharding import Mesh
from jax.sharding import PartitionSpec as P

F32 = jnp.float32
BF16 = jnp.bfloat16
EPS = 1e-06
ROPE_BASE = 1000000.0
NEG = -1e30
HEAD = 128
EXP_SCALE = float(HEAD**-0.5 * np.log2(np.e))
CTX = ("y", "x", "zh")
TP = ("zl", "c")
VMEM = pl.BlockSpec(memory_space=pltpu.VMEM)
SMEM = pl.BlockSpec(memory_space=pltpu.SMEM)
ANY = pl.BlockSpec(memory_space=pl.ANY)
LIMIT = 18 << 20
SCALE = 0.25


def cost(microseconds):
    return pl.CostEstimate(
        flops=int(microseconds * SCALE * 1.1e9), bytes_accessed=1024, transcendentals=0
    )
NN = (((1,), (0,)), ((), ()))
NT = (((1,), (1,)), ((), ()))


def shift(value, axis, size, by):
    return lax.ppermute(value, axis, [(i, (i + by) % size) for i in range(size)])


def rope_tables(positions):
    lane = jnp.arange(HEAD)
    freqs = ROPE_BASE ** ((lane % (HEAD // 2)).astype(F32) * (-2.0 / HEAD))
    angles = positions.astype(F32)[:, None] * freqs[None, :]
    return jnp.cos(angles), jnp.where(lane < HEAD // 2, -1.0, 1.0)[None, :] * jnp.sin(angles)


def head_rope(values, gain, cosine, sine):
    mean_square = jnp.mean(values * values, axis=-1, keepdims=True)
    normed = values * lax.rsqrt(mean_square + EPS) * gain
    return normed * cosine + pltpu.roll(normed, HEAD // 2, 1) * sine


def in_order(blocks, zl, c):
    b0, b1, b2, b3 = blocks
    first, second = jnp.where(c == 0, b0, b1), jnp.where(c == 0, b1, b0)
    third, fourth = jnp.where(c == 0, b2, b3), jnp.where(c == 0, b3, b2)
    low, high = zl == 0, zl != 0
    return (
        jnp.where(low, first, third),
        jnp.where(low, second, fourth),
        jnp.where(high, first, third),
        jnp.where(high, second, fourth),
    )


def scorer_qkv_kernel(
    place_ref, b0, b1, b2, b3, gain_ref, wq_ref, wk_ref, wv_ref, gq_ref, gkv_ref,
    qg_ref, kg_ref, cos_ref, sin_ref, after_ref, out_ref, w_ref, normed_ref,
):
    zl, c = place_ref[0], place_ref[1]
    pair = 2 * HEAD
    for i in range(2):
        mine, got = (
            jnp.where(
                c == 0,
                ref[:, 2 * i * HEAD : (2 * i + 1) * HEAD],
                ref[:, (2 * i + 1) * HEAD : (2 * i + 2) * HEAD],
            )
            for ref in (wq_ref, gq_ref)
        )
        w_ref[:, i * HEAD : (i + 1) * HEAD] = jnp.where(c == 0, mine, got)
        w_ref[:, pair + i * HEAD : pair + (i + 1) * HEAD] = jnp.where(c == 0, got, mine)
    for i, own_ref in ((1, wk_ref), (2, wv_ref)):
        own, got = own_ref[...], gkv_ref[:, (i - 1) * pair : i * pair]
        w_ref[:, 2 * i * pair : (2 * i + 1) * pair] = jnp.where(c == 0, own, got)
        w_ref[:, (2 * i + 1) * pair : (2 * i + 2) * pair] = jnp.where(c == 0, got, own)
    step, many = 128, b0.shape[0]
    half = many // 2
    for part in range(many // step):
        rows = slice(part * step, (part + 1) * step)
        blocks = in_order([b[rows, :].astype(F32) for b in (b0, b1, b2, b3)], zl, c)
        states = jnp.concatenate(blocks, axis=1)
        mean_square = jnp.mean(states * states, axis=-1, keepdims=True)
        normed = (states * lax.rsqrt(mean_square + EPS) * gain_ref[...]).astype(BF16)
        normed_ref[rows, :] = normed
        mixed = lax.dot_general(normed, w_ref[:, : 2 * pair], NN, preferred_element_type=F32)
        for h in range(4):
            turned = head_rope(
                mixed[:, h * HEAD : (h + 1) * HEAD], qg_ref[...], cos_ref[rows, :], sin_ref[rows, :]
            )
            out_ref[h, many + part * step : many + (part + 1) * step, :] = turned.T.astype(BF16)
    for part in range(half // step):
        rows = pl.ds(pl.multiple_of(c * half + part * step, step), step)
        mixed = lax.dot_general(
            normed_ref[rows, :], w_ref[:, 2 * pair :], NN, preferred_element_type=F32
        )
        for h in range(4):
            key = head_rope(
                mixed[:, h * HEAD : (h + 1) * HEAD], kg_ref[...], cos_ref[rows, :], sin_ref[rows, :]
            )
            out_ref[h, part * step : (part + 1) * step, :] = key.astype(BF16)
            value = mixed[:, (4 + h) * HEAD : (5 + h) * HEAD].T
            out_ref[h, half + part * step : half + (part + 1) * step, :] = value.astype(BF16)


def scorer_qkv(place, blocks, *rest):
    rows = blocks[0].shape[0]
    return pl.pallas_call(
        scorer_qkv_kernel,
        out_shape=jax.ShapeDtypeStruct((4, 2 * rows, HEAD), BF16),
        in_specs=[SMEM] + [VMEM] * (3 + len(rest)) + [ANY],
        out_specs=VMEM,
        scratch_shapes=[
            pltpu.VMEM((4 * blocks[0].shape[1], 12 * HEAD), BF16),
            pltpu.VMEM((rows, 4 * blocks[0].shape[1]), BF16),
        ],
        compiler_params=pltpu.CompilerParams(vmem_limit_bytes=LIMIT),
        cost_estimate=cost(7),
        name="scorer_qkv",
    )(place, *blocks, *rest)


def project_kernel(place_ref, a0, a1, a2, a3, w_ref, got_ref, *refs):
    away_out, home_out, pick_ref = refs[-3:]
    y, c = place_ref[0], place_ref[1]
    heads = [None] * 4
    for i in range(2):
        mine, got = (
            jnp.where(
                c == 0,
                ref[2 * i * HEAD : (2 * i + 1) * HEAD, :],
                ref[(2 * i + 1) * HEAD : (2 * i + 2) * HEAD, :],
            )
            for ref in (w_ref, got_ref)
        )
        heads[i] = jnp.where(c == 0, mine, got)
        heads[2 + i] = jnp.where(c == 0, got, mine)
    width = w_ref.shape[1] // 4
    for at in range(4):
        slot = lax.rem(y - at + 4, 4)
        for block in range(4):
            pick_ref[block, pl.ds(pl.multiple_of(slot * HEAD, HEAD), HEAD), :] = heads[at][
                :, block * width : (block + 1) * width
            ]
    attended = jnp.concatenate([a[...] for a in (a0, a1, a2, a3)], axis=1)
    for zl in range(2):
        away_out[zl] = lax.dot_general(
            attended, pick_ref[zl * 2 + 1 - c], NN, preferred_element_type=F32
        ).astype(BF16)
        home_out[zl] = lax.dot_general(attended, pick_ref[zl * 2 + c], NN, preferred_element_type=F32)


def project(place, attended, weight, got, after):
    rows, width = attended[0].shape[0], weight.shape[1] // 4
    return pl.pallas_call(
        project_kernel,
        out_shape=[
            jax.ShapeDtypeStruct((2, rows, width), BF16),
            jax.ShapeDtypeStruct((2, rows, width), F32),
        ],
        in_specs=[SMEM] + [VMEM] * 6 + [ANY] * len(after),
        out_specs=[VMEM] * 2,
        scratch_shapes=[pltpu.VMEM((4, 4 * HEAD, width), BF16)],
        compiler_params=pltpu.CompilerParams(vmem_limit_bytes=LIMIT),
        cost_estimate=cost(2.5),
        name="scorer_project",
    )(place, *attended, weight, got, *after)


SLOTS = 8


def route_kernel(place_ref, counts_ref, order_ref, rows_ref, embeds_ref, sent_out, select_out):
    place = place_ref[0]
    shards, capacity = counts_ref.shape[0], rows_ref.shape[1]
    turns, entries = capacity // shards, sent_out.shape[0]
    iota = lambda shape, axis: lax.broadcasted_iota(jnp.int32, shape, axis)
    square = (shards, shards)
    counts = counts_ref[...]
    eye = iota(square, 0) == iota(square, 1)
    rank_row = jnp.sum(
        jnp.where(order_ref[...] == iota(square, 1), iota(square, 0), 0), axis=0, keepdims=True
    )
    rank = jnp.sum(jnp.where(eye, rank_row, 0), axis=1, keepdims=True)
    count_row = jnp.sum(jnp.where(eye, counts, 0), axis=0, keepdims=True)
    starts = jnp.sum(jnp.where(rank_row < rank, count_row, 0), axis=1, keepdims=True)
    my_start = jnp.sum(jnp.where(iota((shards, 1), 0) == place, starts, 0))
    entry = iota((entries, 1), 0)
    slot = ((entry // SLOTS - my_start) & (shards - 1)) + shards * (entry % SLOTS)
    picked = jnp.sum(
        jnp.where(iota((entries, capacity), 1) == slot, rows_ref[...], 0), axis=1, keepdims=True
    )
    pick = jnp.where(iota((entries, embeds_ref.shape[0]), 1) == picked, 1.0, 0.0).astype(BF16)
    sent_out[...] = lax.dot_general(
        pick, embeds_ref[...], NN, preferred_element_type=F32
    ).astype(BF16)
    wide = (shards, entries)
    source = iota(wide, 0) == iota(wide, 1) // SLOTS
    start = jnp.sum(jnp.where(source, starts, 0), axis=0, keepdims=True)
    count = jnp.sum(jnp.where(source, counts, 0), axis=0, keepdims=True)
    turn = iota((1, entries), 1) % SLOTS
    within = ((place - start) & (shards - 1)) + shards * turn
    good = (within < count) & (turn < turns)
    turn_at = (start + within) // shards
    dest = jnp.where(good, turn_at // 3 * SLOTS + turn_at % 3, -1)
    select_out[...] = jnp.where(iota(select_out.shape, 0) == dest, 1.0, 0.0).astype(BF16)


def route(place, counts, order, rows, embeds):
    entries = rows.shape[0] * counts.shape[0] * SLOTS
    return pl.pallas_call(
        route_kernel,
        out_shape=[
            jax.ShapeDtypeStruct((entries, embeds.shape[1]), BF16),
            jax.ShapeDtypeStruct((entries, entries), BF16),
        ],
        in_specs=[SMEM] + [VMEM] * 4,
        out_specs=[VMEM] * 2,
        compiler_params=pltpu.CompilerParams(vmem_limit_bytes=LIMIT),
        cost_estimate=cost(1),
        name="route",
    )(place, counts, order, rows, embeds)


def place_kernel(select_ref, rows_ref, after_ref, out_ref):
    out_ref[...] = lax.dot_general(
        select_ref[...], rows_ref[...], NN, preferred_element_type=F32
    ).astype(BF16)


def land_kernel(rows_ref, after_ref, out_ref):
    shape = (out_ref.shape[0], rows_ref.shape[0])
    shards = shape[1] // SLOTS
    row, entry = lax.broadcasted_iota(jnp.int32, shape, 0), lax.broadcasted_iota(jnp.int32, shape, 1)
    wanted = (row % shards) * SLOTS + row // shards
    select = jnp.where(entry == wanted, 1.0, 0.0).astype(BF16)
    out_ref[...] = lax.dot_general(
        select, rows_ref[...], NN, preferred_element_type=F32
    ).astype(BF16)


def move(kernel, name, rows, *operands):
    return pl.pallas_call(
        kernel,
        out_shape=jax.ShapeDtypeStruct((rows, operands[-2].shape[1]), BF16),
        in_specs=[VMEM] * (len(operands) - 1) + [ANY],
        out_specs=VMEM,
        compiler_params=pltpu.CompilerParams(vmem_limit_bytes=LIMIT),
        cost_estimate=cost(0.5),
        name=name,
    )(*operands)


def split_kernel(b0, b1, b2, b3, after_ref, own_out, query_out):
    size = own_out.shape[1]
    for at, ref in enumerate((b0, b1, b2, b3)):
        own_out[at] = ref[:size, :]
        query_out[at] = ref[size:, :]


def split(blocks, after):
    size = blocks[0].shape[0] // 2
    return pl.pallas_call(
        split_kernel,
        out_shape=[jax.ShapeDtypeStruct((4, size, HEAD), BF16)] * 2,
        in_specs=[VMEM] * 4 + [ANY],
        out_specs=[VMEM] * 2,
        cost_estimate=cost(40),
        name="split",
    )(*blocks, after)


def attend_kernel(first, last, many, waits, *refs):
    place_ref, qa_ref, qb_ref = refs[:3]
    chunk_refs, refs = refs[3 : 3 + many], refs[3 + many :]
    carried = None
    if not first:
        carried, refs = refs[:3], refs[3:]
    refs = refs[waits:]
    if last:
        mine_out, *theirs_out = refs[:3]
        refs = refs[3:]
    m_ref, l_ref, a_ref, k_ref, vt_ref, q_ref = refs
    y, c = place_ref[0], place_ref[1]
    size = qa_ref.shape[1]
    half = size // 2
    wide = half * many
    for block in range(4):
        slot = lax.rem(y - block + 4, 4)
        for at, ref in enumerate(chunk_refs):
            chunk = ref[slot]
            k_ref[(block * many + at) * half : (block * many + at + 1) * half, :] = chunk[:half]
            for i in range(half // HEAD):
                lanes = (block * many + at) * half + i * HEAD
                vt_ref[:, lanes : lanes + HEAD] = chunk[half + i * HEAD : half + (i + 1) * HEAD]
        for i in range(size // HEAD):
            tile = slice(i * HEAD, (i + 1) * HEAD)
            q_ref[block, :, tile] = qa_ref[slot, tile, :]
            q_ref[block, :, size + i * HEAD : size + (i + 1) * HEAD] = qb_ref[slot, tile, :]

    def scores(step):
        block, begin, end, _ = step
        return lax.dot_general(k_ref[begin:end, :], q_ref[block], NN, preferred_element_type=F32)

    def run(steps, source):
        state = {}
        ahead = scores(steps[0])
        for at, (block, begin, end, masked) in enumerate(steps):
            s = ahead
            if at + 1 < len(steps):
                ahead = scores(steps[at + 1])
            if masked:
                shape = (s.shape[0], size)
                key_at = lax.broadcasted_iota(jnp.int32, shape, 0) + c * half
                allowed = key_at <= lax.broadcasted_iota(jnp.int32, shape, 1)
                s = jnp.where(jnp.concatenate([allowed, allowed], axis=1), s, NEG)
            if block not in state and source is not None:
                state[block] = tuple(ref[block] for ref in source)
            fresh = jnp.max(s, axis=0, keepdims=True)
            if block in state:
                m, l, a = state[block]
                fresh = jnp.maximum(m, fresh)
                shrink = jnp.exp2((m - fresh) * EXP_SCALE)
            weights = jnp.exp2(s * EXP_SCALE - fresh * EXP_SCALE)
            total = jnp.sum(weights, axis=0, keepdims=True)
            added = lax.dot_general(
                vt_ref[:, begin:end], weights.astype(BF16), NN, preferred_element_type=F32
            )
            if block in state:
                total, added = l * shrink + total, a * shrink + added
            state[block] = (fresh, total, added)
        for block, values in state.items():
            m_ref[block], l_ref[block], a_ref[block] = values

    def earlier(block):
        end = block * wide
        return [(block, at, min(at + 512, end), False) for at in range(0, end, 512)]

    def same(block, at):
        begin = block * wide + at * half
        return [(block, begin, begin + half, first)]

    if first:
        run(sum([earlier(block) + same(block, 0) for block in range(4)], []), None)
    else:
        for ref, out in zip(carried, (m_ref, l_ref, a_ref)):
            out[0] = ref[0]
        run(sum([earlier(block) for block in range(1, 4)], []), carried)
        for at in range(many):
            for odd in range(2):

                @pl.when(place_ref[2 + 2 * at + odd] > 0)
                def _():
                    run(same(odd, at) + same(odd + 2, at), (m_ref, l_ref, a_ref))

    if last:
        for head in range(2):
            lanes = slice(head * size, (head + 1) * size)
            for block in range(4):
                out = mine_out.at[block] if head == 0 else theirs_out[block // 2].at[block % 2]
                out[:HEAD, :] = a_ref[block, :, lanes]
                out[HEAD : HEAD + 1, :] = m_ref[block, :, lanes]
                out[HEAD + 1 : HEAD + 2, :] = l_ref[block, :, lanes]
                out[HEAD + 2 :, :] = jnp.zeros((6, size), F32)


def attend(first, last, place, queries, chunks, carry, after):
    many, size = len(chunks), queries[0].shape[1]
    state = [(4, 1, 2 * size), (4, 1, 2 * size), (4, HEAD, 2 * size)]
    keys = 4 * many * size // 2
    scratch = [pltpu.VMEM((keys, HEAD), BF16), pltpu.VMEM((HEAD, keys), BF16)]
    scratch.append(pltpu.VMEM((4, HEAD, 2 * size), BF16))
    if last:
        out_shape = [jax.ShapeDtypeStruct((many, HEAD + 8, size), F32) for many in (4, 2, 2)]
        scratch = [pltpu.VMEM(s, F32) for s in state] + scratch
    else:
        out_shape = [jax.ShapeDtypeStruct(s, F32) for s in state]
    carry = () if first else carry
    at = 3 + many

    def kernel(*refs):
        attend_kernel(first, last, many, len(after), *refs)

    return pl.pallas_call(
        kernel,
        out_shape=out_shape,
        in_specs=[SMEM] + [VMEM] * (2 + many + len(carry)) + [ANY] * len(after),
        out_specs=[VMEM] * len(out_shape),
        scratch_shapes=scratch,
        input_output_aliases={} if first or last else {at: 0, at + 1: 1, at + 2: 2},
        compiler_params=pltpu.CompilerParams(vmem_limit_bytes=LIMIT),
        cost_estimate=cost(4.5 * many),
        name="scorer_attend",
    )(place, *queries, *chunks, *carry, *after)


def merge_kernel(mine_ref, first_ref, second_ref, *refs):
    out_ref = refs[-1]
    for block in range(4):
        mine = mine_ref.at[block]
        got = (first_ref, second_ref)[block // 2].at[block % 2]
        m0, m1 = mine[HEAD : HEAD + 1, :], got[HEAD : HEAD + 1, :]
        top = jnp.maximum(m0, m1)
        f0, f1 = jnp.exp2((m0 - top) * EXP_SCALE), jnp.exp2((m1 - top) * EXP_SCALE)
        total = mine[HEAD + 1 : HEAD + 2, :] * f0 + got[HEAD + 1 : HEAD + 2, :] * f1
        mixed = mine[:HEAD, :] * f0 + got[:HEAD, :] * f1
        out_ref[block] = (mixed / total).T.astype(BF16)


def merge(mine, first, second, after):
    size = mine.shape[2]
    return pl.pallas_call(
        merge_kernel,
        out_shape=jax.ShapeDtypeStruct((4, size, HEAD), BF16),
        in_specs=[VMEM] * 3 + [ANY] * len(after),
        out_specs=VMEM,
        compiler_params=pltpu.CompilerParams(vmem_limit_bytes=LIMIT),
        cost_estimate=cost(1.5),
        name="merge",
    )(mine, first, second, *after)


def target_qkv_kernel(
    place_ref, b0, b1, b2, b3, gain_ref, qg_ref, kg_ref, cos_ref, sin_ref, wq_ref, wk_ref, wv_ref,
    *refs,
):
    q_out, kv_out, normed_ref, q_acc, k_acc, v_acc = refs[-6:]
    at = pl.program_id(0)
    steps = pl.num_programs(0)
    rows, part = b0.shape
    block = wq_ref.shape[0]

    @pl.when(at == 0)
    def _():
        blocks = in_order([b[...].astype(F32) for b in (b0, b1, b2, b3)], place_ref[0], place_ref[1])
        total = sum(jnp.sum(b * b, axis=-1, keepdims=True) for b in blocks)
        factor = lax.rsqrt(total / (4 * part) + EPS)
        for index in range(4):
            normed = blocks[index] * factor * gain_ref[:, index * part : (index + 1) * part]
            normed = normed.astype(BF16)
            for piece in range(part // block):
                normed_ref[index * (part // block) + piece] = normed[
                    :, piece * block : (piece + 1) * block
                ]
        q_acc[...] = jnp.zeros_like(q_acc)
        k_acc[...] = jnp.zeros_like(k_acc)
        v_acc[...] = jnp.zeros_like(v_acc)

    normed = normed_ref[at]
    q_acc[...] += lax.dot_general(normed, wq_ref[...], NN, preferred_element_type=F32)
    k_acc[...] += lax.dot_general(normed, wk_ref[...], NN, preferred_element_type=F32)
    v_acc[...] += lax.dot_general(normed, wv_ref[...], NN, preferred_element_type=F32)

    @pl.when(at == steps - 1)
    def _():
        cosine, sine = cos_ref[...], sin_ref[...]
        for h in range(8):
            turned = head_rope(q_acc[:, h * HEAD : (h + 1) * HEAD], qg_ref[...], cosine, sine)
            q_out[h // 4, (h % 4) * rows : (h % 4 + 1) * rows, :] = turned.astype(BF16)
        for h in range(2):
            lanes = slice(h * HEAD, (h + 1) * HEAD)
            turned = head_rope(k_acc[:, lanes], kg_ref[...], cosine, sine)
            kv_out[:, lanes] = turned.astype(BF16)
        kv_out[:, 2 * HEAD :] = v_acc[...].astype(BF16)


def target_qkv(place, blocks, gain, query_gain, key_gain, cosine, sine, wq, wk, wv, after):
    rows, part = blocks[0].shape
    block = 640
    steps = 4 * part // block
    whole = lambda shape: pl.BlockSpec(shape, lambda i: (0,) * len(shape))
    return pl.pallas_call(
        target_qkv_kernel,
        grid=(steps,),
        out_shape=[
            jax.ShapeDtypeStruct((2, 4 * rows, HEAD), BF16),
            jax.ShapeDtypeStruct((rows, 4 * HEAD), BF16),
        ],
        in_specs=[SMEM]
        + [whole((rows, part))] * 4
        + [whole(gain.shape), whole((1, HEAD)), whole((1, HEAD)), whole((rows, HEAD)), whole((rows, HEAD))]
        + [
            pl.BlockSpec((block, wq.shape[1]), lambda i: (i, 0)),
            pl.BlockSpec((block, wk.shape[1]), lambda i: (i, 0)),
            pl.BlockSpec((block, wv.shape[1]), lambda i: (i, 0)),
        ]
        + [ANY] * len(after),
        out_specs=[whole((2, 4 * rows, HEAD)), whole((rows, 4 * HEAD))],
        scratch_shapes=[
            pltpu.VMEM((steps, rows, block), BF16),
            pltpu.VMEM((rows, wq.shape[1]), F32),
            pltpu.VMEM((rows, wk.shape[1]), F32),
            pltpu.VMEM((rows, wv.shape[1]), F32),
        ],
        compiler_params=pltpu.CompilerParams(vmem_limit_bytes=LIMIT),
        cost_estimate=cost(6.5),
        name="target_qkv",
    )(place, *blocks, gain, query_gain, key_gain, cosine, sine, wq, wk, wv, *after)


def target_attend_kernel(place_ref, q_ref, c0, c1, c2, c3, after_ref, out_ref, m_ref, l_ref, a_ref):
    y, x, zh = place_ref[0], place_ref[1], place_ref[2]
    members = 4
    rows = q_ref.shape[1] // members

    def chunk(keys_ref, own):
        for g in range(2):
            keys = keys_ref[:, g * HEAD : (g + 1) * HEAD]
            values = keys_ref[:, (2 + g) * HEAD : (3 + g) * HEAD]
            s = lax.dot_general(q_ref[g], keys, NT, preferred_element_type=F32)
            if own:
                row = lax.broadcasted_iota(jnp.int32, (rows, s.shape[1]), 0) + (2 * x + zh) * rows
                key_at = lax.broadcasted_iota(jnp.int32, (rows, s.shape[1]), 1)
                allowed = jnp.concatenate([key_at <= row] * members, axis=0)
                s = jnp.where(allowed, s, NEG)
            fresh = jnp.max(s, axis=1, keepdims=True)
            if not own:
                m = m_ref[g]
                fresh = jnp.maximum(m, fresh)
                shrink = jnp.exp2((m - fresh) * EXP_SCALE)
            weights = jnp.exp2(s * EXP_SCALE - fresh * EXP_SCALE)
            total = jnp.sum(weights, axis=1, keepdims=True)
            added = lax.dot_general(weights.astype(BF16), values, NN, preferred_element_type=F32)
            if not own:
                total, added = l_ref[g] * shrink + total, a_ref[g] * shrink + added
            m_ref[g], l_ref[g], a_ref[g] = fresh, total, added

    chunk(c0, True)
    for by, ref in ((1, c1), (2, c2), (3, c3)):

        @pl.when(y >= by)
        def _():
            chunk(ref, False)

    for g in range(2):
        context = (a_ref[g] / l_ref[g]).astype(BF16)
        for member in range(members):
            lanes = slice((g * members + member) * HEAD, (g * members + member + 1) * HEAD)
            out_ref[:, lanes] = context[member * rows : (member + 1) * rows]


def target_attend(place, queries, chunks, after):
    groups, many, _ = queries.shape
    rows = many // 4
    return pl.pallas_call(
        target_attend_kernel,
        out_shape=jax.ShapeDtypeStruct((rows, 8 * HEAD), BF16),
        in_specs=[SMEM] + [VMEM] * 5 + [ANY],
        out_specs=VMEM,
        scratch_shapes=[
            pltpu.VMEM((groups, many, 1), F32),
            pltpu.VMEM((groups, many, 1), F32),
            pltpu.VMEM((groups, many, HEAD), F32),
        ],
        compiler_params=pltpu.CompilerParams(vmem_limit_bytes=LIMIT),
        cost_estimate=cost(6),
        name="target_attend",
    )(place, queries, *chunks, after)


def gather_tp(value, hops):
    chip = shift(value, "zl", 2, 1)
    if hops == 2:
        return [value, shift(value, "c", 2, 1), chip, shift(chip, "c", 2, 1)]
    away = [(i, i ^ 3) for i in range(4)]
    return [value, shift(value, "c", 2, 1), chip, lax.ppermute(value, TP, away)]


def exchange_y(blocks, y):
    got = [lax.dynamic_index_in_dim(blocks, y, 0, keepdims=False)]
    for by in (1, 2, 3):
        block = lax.dynamic_index_in_dim(blocks, lax.rem(y + by, 4), 0, keepdims=False)
        pairs = [
            (4 * i + j, (i + by) % 4 * 4 + (3 - j if by % 2 else j)) for i in range(4) for j in range(4)
        ]
        got.append(lax.ppermute(block, ("y", "x"), pairs))
    return got


def on_device(
    prompt_states,
    scorer_gain,
    scorer_query,
    scorer_key,
    scorer_value,
    scorer_querynorm,
    scorer_keynorm,
    scorer_project,
    target_embeds,
    target_gain,
    target_query,
    target_key,
    target_value,
    target_querynorm,
    target_keynorm,
    kept_rows,
    kept_counts,
    shard_order,
):
    y, x, zh, zl, c = (lax.axis_index(name) for name in ("y", "x", "zh", "zl", "c"))
    place = (y * 4 + x) * 2 + zh
    tp_place = jnp.stack([zl, c]).astype(jnp.int32)
    rows = prompt_states.shape[0]

    state_blocks = gather_tp(prompt_states, 1)
    weights = (scorer_query, scorer_key, scorer_value)
    got_weights = [
        shift(scorer_query, "c", 2, 1),
        shift(jnp.concatenate([scorer_key, scorer_value], axis=1), "c", 2, 1),
    ]
    got_project = shift(scorer_project, "c", 2, 1)
    cosine, sine = rope_tables(place * rows + jnp.arange(rows, dtype=jnp.int32))
    shards = shard_order.shape[0]
    features = target_embeds.shape[1]
    target_rows = kept_rows.shape[1] // 2
    counts = lax.all_to_all(jnp.broadcast_to(kept_counts[:, None], (shards, 1)), CTX, 0, 0, tiled=True)
    def exchange_rows(value):
        value = lax.all_to_all(value.reshape(shards, SLOTS, features), CTX, 0, 0, tiled=True)
        return value.reshape(shards * SLOTS, features)

    sent, select = route(
        place[None].astype(jnp.int32), counts, shard_order[:, None], kept_rows, target_embeds
    )
    mixed = scorer_qkv(
        tp_place, state_blocks, scorer_gain[None], *weights, *got_weights,
        scorer_querynorm[None], scorer_keynorm[None], cosine, sine, sent,
    )
    exchanged = exchange_y(mixed, y)
    placed = move(place_kernel, "place", shards * SLOTS, select, exchange_rows(sent), mixed)

    own, query = split(exchanged, placed)
    compressed = move(land_kernel, "land", target_rows, exchange_rows(placed), own)
    queries = (query, shift(query, "c", 2, 1))

    def chunk_from(by, flip):
        pairs = [
            (2 * i + j, (i + by) % 4 * 2 + (j + flip) % 2) for i in range(4) for j in range(2)
        ]
        return lax.ppermute(own, ("x", "zh"), pairs)

    def relations(by, flip):
        if by == 0:
            return [2 * zh - 1] * 2
        ahead = x - lax.rem(x - by + 4, 4)
        even = jnp.where(y % 2 == 0, ahead, -ahead)
        return [even, -even]

    def call(last, places, chunks, carry, after):
        scalars = jnp.stack([y, c] + sum([relations(*at) for at in places], [])).astype(jnp.int32)
        return attend(carry is None, last, scalars, queries, chunks, carry, after)

    near = [(0, 1), (1, 0), (3, 0), (2, 0)]
    far = [(1, 1), (3, 1), (2, 1)]
    near_chunks = [chunk_from(*at) for at in near]
    far_chunks = [shift(near_chunks[0], "x", 4, at[0]) for at in far]
    carry = call(False, [], [own], None, [compressed, got_project])

    target_cos, target_sin = rope_tables(place * target_rows + jnp.arange(target_rows, dtype=jnp.int32))
    target_queries, target_kv = target_qkv(
        tp_place, gather_tp(compressed, 2), target_gain[None], target_querynorm[None], target_keynorm[None],
        target_cos, target_sin, target_query, target_key, target_value, [],
    )
    carry = call(False, near, near_chunks, carry, [target_kv])

    line = lax.all_to_all(
        jnp.broadcast_to(target_kv, (8, *target_kv.shape)), ("x", "zh"), 0, 0, tiled=True
    ).reshape(8 * target_rows, -1)
    mine, *theirs = call(True, far, far_chunks, carry, [line])
    chunks = [line] + [
        lax.ppermute(line, "y", [(i, i + by) for i in range(4 - by)]) for by in (1, 2, 3)
    ]
    attended = merge(mine, *(shift(half, "c", 2, 1) for half in theirs), chunks[1:])

    away, home = project(
        jnp.stack([y, c]).astype(jnp.int32), exchange_y(attended, y), scorer_project, got_project, []
    )
    summed = home + shift(away, "c", 2, 1).astype(F32)
    leaving = lax.dynamic_index_in_dim(summed, 1 - zl, 0, keepdims=False).astype(BF16)
    staying = lax.dynamic_index_in_dim(summed, zl, 0, keepdims=False)
    scorer_states = (staying + shift(leaving, "zl", 2, 1).astype(F32)).astype(BF16)

    target_place = jnp.stack([y, x, zh]).astype(jnp.int32)
    target_context = target_attend(target_place, target_queries, chunks, away)
    return (scorer_states, target_context)


def solution(mesh):
    fine = Mesh(mesh.devices.reshape(4, 4, 2, 2, 2), CTX + TP)
    return jax.shard_map(
        on_device,
        mesh=fine,
        in_specs=(
            P(CTX, TP),
            P(),
            P(None, TP),
            P(None, TP),
            P(None, TP),
            P(),
            P(),
            P(TP, None),
            P(CTX, TP),
            P(),
            P(None, TP),
            P(None, TP),
            P(None, TP),
            P(),
            P(),
            P(CTX, None),
            P(CTX),
            P(),
        ),
        out_specs=(P(CTX, TP), P(CTX, TP)),
        check_vma=False,
    )
```
